32 devices in a mesh: lat: 4 (over z), lon: 8 (over y, x, core).
Axes of the slice: x: 2, y: 2, z: 4, core: 2. Of those that a mesh axis runs over, the one named last changes fastest.
Arguments:
- east_courant: float32 [2, 16, 384, 1024], P(None, None, 'lat', 'lon'), may hold values from 0.3 to 400
- north_courant: float32 [2, 16, 384, 1024], P(None, None, 'lat', 'lon'), may hold values from -0.45 to 0.45
- kernels: float32 [2, 16, 8192], P(None, None, ('lat', 'lon')), may hold values from 0.1 to 1.2
- departures: float32 [2, 2, 8192], P(None, None, ('lat', 'lon')), may hold values from -6 to 6
- cells: int32 [2, 8192], P(None, ('lat', 'lon')), may hold values from 0 to 12287
- counts: int32 [2, 1024], P(None, ('lat', 'lon')), may hold values from 1 to 8, as said below
Outputs:
- adjoint_state: float32 [2, 16, 384, 1024], P(None, None, 'lat', 'lon')
- flux_gradient: float32 [2, 384, 1024], P(None, 'lat', 'lon')
The draws below stay inside these ranges and needn't reach their ends.
Inputs may be any that keep to these rules, and one draw needn't show every extreme that they name: counts[n, s * 32 + o] is the number of live slots from device s to owner o in step n; in every step some owner receives 8 from every device. `cells`: a cell of the owner's block, row-major over 96 x 128.
All inputs are finite; a program needn't handle non-finite values.
Results may differ from the reference program's by a relative error of at most 0.0003.
Values sent between devices are 32-bit elements; how exact they have to be, the bound alone decides.
A program may use at most 192 MiB of HBM per device.

```python
import math
import jax
import jax.numpy as jnp
from jax import lax

TR = 2
LEV = 16
CLAT = 96
CLON = 128
STEPS = 2
CAP = 8
OWNERS = 32
NLAT = 384
NLON = 1024
SLOTS = 8192
N_LON = 8


def draw_east_courant(key, part):
    unit_draw = jax.random.uniform(key, (STEPS, LEV, NLAT, NLON), jnp.float32)
    low_log = math.log(0.301)
    high_log = math.log(60.0)
    return jnp.exp(low_log + (high_log - low_log) * unit_draw)


def draw_departures(key, part):
    noise = jax.random.normal(key, (STEPS, TR, SLOTS), jnp.float32)
    value_draw = noise
    return jnp.clip(value_draw, -6.0, 6.0)


def draw_counts(key, part):
    key_busy, key_quiet, key_heavy, key_full = jax.random.split(key, 4)
    busy_owner = jax.random.randint(key_busy, (STEPS, 1, OWNERS), 0, 4) == 0
    quiet_draw = jax.random.randint(key_quiet, (STEPS, OWNERS, OWNERS), 1, CAP // 2 + 1)
    heavy_draw = jax.random.randint(key_heavy, (STEPS, OWNERS, OWNERS), CAP // 2, CAP + 1)
    full_owner = jax.random.randint(key_full, (STEPS, 1, 1), 0, OWNERS)
    destination = lax.broadcasted_iota(jnp.int32, (STEPS, OWNERS, OWNERS), 2)
    count_draw = jnp.where(busy_owner, heavy_draw, quiet_draw)
    count_draw = jnp.where(destination == full_owner, CAP, count_draw)
    return count_draw.reshape(STEPS, OWNERS * OWNERS).astype(jnp.int32)


def place_ends(result, rng, low, high):
    longest = result.shape.index(max(result.shape))
    spots = []
    for shift in (0, 1):
        where = [jax.random.randint(jax.random.fold_in(rng, axis), (), 0, length) for axis, length in enumerate(result.shape)]
        where[longest] = (where[longest] + shift) % result.shape[longest]
        spots.append(tuple(where))
    return result.at[spots[0]].set(low).at[spots[1]].set(high)


def block_scale(stream_key, extent, cuts, low, high):
    factor_of = 1.0
    for position, shards_of in cuts:
        heights = jax.random.uniform(jax.random.fold_in(jax.random.fold_in(stream_key, 6), position), (shards_of,), jnp.float32, low / len(cuts), high / len(cuts))
        factor_of = factor_of * jnp.repeat(jnp.exp(heights), extent[position] // shards_of).reshape((-1,) + (1,) * (len(extent) - 1 - position))
    return factor_of


def setup_inputs(seed: int = 0) -> dict:
    key_of = jax.random.split(jax.random.key(seed), 7)
    east_courant = draw_east_courant(jax.random.fold_in(key_of[6], 71), 0)
    north_courant = jnp.clip(jax.random.uniform(key_of[1], (STEPS, LEV, NLAT, NLON), jnp.float32, -0.45, 0.45) * block_scale(key_of[1], (STEPS, LEV, NLAT, NLON), ((2, 4), (3, 8)), -0.4, 0.0), -0.45, 0.45)
    kernels = jnp.clip(0.1 + 1.1 * jax.random.uniform(key_of[2], (STEPS, LEV, SLOTS), jnp.float32) ** block_scale(key_of[2], (STEPS, LEV, SLOTS), ((2, 32),), -0.2, 0.2), 0.1, 1.2)
    departures = draw_departures(jax.random.fold_in(key_of[6], 71), 0)
    cells = place_ends(jax.random.randint(key_of[4], (STEPS, SLOTS), 0, CLAT * CLON), jax.random.fold_in(key_of[4], 1), 0, (CLAT * CLON) - 1).astype(jnp.int32)
    counts = draw_counts(jax.random.fold_in(key_of[6], 71), 0)
    return dict(east_courant=east_courant, north_courant=north_courant, kernels=kernels, departures=departures, cells=cells, counts=counts)


def compose(outer_map, inner_map):
    return (outer_map[0] * inner_map[0], outer_map[0] * inner_map[1] + outer_map[1])


def reverse_pair(higher, lower_map):
    return compose(lower_map, higher)


def cyclic_solve(retain, source, along):
    affine = lax.associative_scan(reverse_pair, (retain, source), reverse=True, axis=along)
    first_gain = lax.slice_in_dim(affine[0], 0, 1, axis=along)
    first_rest = lax.slice_in_dim(affine[1], 0, 1, axis=along)
    closure = first_rest / (1.0 - first_gain)
    return affine[0] * closure + affine[1]


def forcing(kernels, departures, cells, counts):
    slot_index = jnp.arange(SLOTS, dtype=jnp.int32)
    per_source = OWNERS * CAP
    source = slot_index // per_source
    owner = (slot_index % per_source) // CAP
    within = slot_index % CAP
    live_slot = within < counts[source * OWNERS + owner]
    lat_cell = (owner // N_LON) * CLAT + cells // CLON
    lon_cell = (owner % N_LON) * CLON + cells % CLON
    flat_cell = (lat_cell * NLON + lon_cell).astype(jnp.int32)
    values = departures * live_slot.astype(departures.dtype)
    terms = values[:, None, :] * kernels[None, :, :]
    field = jnp.zeros((TR, LEV, NLAT * NLON), jnp.float32).at[:, :, flat_cell].add(terms)
    return field.reshape(TR, LEV, NLAT, NLON)


def lat_adjoint(adjoint, north):
    lat_rows = north.shape[1]
    top_row = lax.broadcasted_iota(jnp.int32, north.shape, 1) == lat_rows - 1
    north_faces = jnp.where(top_row, 0.0, north)
    northward = jnp.maximum(north_faces, 0.0)
    southward = jnp.minimum(north_faces, 0.0)
    padded = jnp.pad(adjoint, ((0, 0), (0, 0), (1, 1), (0, 0)))
    upper_row = padded[:, :, 2:]
    lower_row = padded[:, :, :-2]
    south_faces = jnp.pad(southward, ((0, 0), (1, 0), (0, 0)))[:, :-1]
    return adjoint + northward * (upper_row - adjoint) + south_faces * (adjoint - lower_row)


def lon_adjoint(adjoint, east):
    retain = east / (1.0 + east)
    weight = 1.0 / (1.0 + east)

    def one_level(inputs):
        level_state, level_retain, level_weight = inputs
        return cyclic_solve(jnp.broadcast_to(level_retain, level_state.shape), level_weight * level_state, 2)

    moved = lax.map(one_level, (jnp.swapaxes(adjoint, 0, 1), retain, weight))
    return jnp.swapaxes(moved, 0, 1)


def reference(east_courant, north_courant, kernels, departures, cells, counts):
    adjoint = jnp.zeros((TR, LEV, NLAT, NLON), jnp.float32)
    flux_gradient = jnp.zeros((TR, NLAT, NLON), jnp.float32)
    for window_step in range(STEPS - 1, -1, -1):
        adjoint = adjoint + forcing(kernels[window_step], departures[window_step], cells[window_step], counts[window_step])
        flux_gradient = flux_gradient + adjoint[:, 0]
        adjoint = lat_adjoint(adjoint, north_courant[window_step])
        adjoint = lon_adjoint(adjoint, east_courant[window_step])
    return adjoint, flux_gradient
```

```python
import functools

import jax
import jax.numpy as jnp
from jax import lax
from jax.experimental import pallas as pl
from jax.experimental.pallas import tpu as pltpu
from jax.sharding import PartitionSpec as P

MESH = pl.DeviceIdType.MESH
SUB = 8
LANES = 128
PAD = 8
F32 = jnp.float32
BF16 = jnp.bfloat16


def kernel(
    dims,
    east_hbm, north_hbm, kern_ref, dep_ref, cells_ref, counts_ref,
    out_ref, flux_ref,
    weight, faces, gain_t, gain_levels, field, rows, rows_t, forcing,
    features, sent, stage_lon, stage_lat, got_t, term_hi, term_lo, left, onehot,
    edge_out, edge_in, face_out, face_in, gain_all, rest_all,
    local_sem, lon_send, lon_recv, lat_send, lat_recv, gain_send, gain_recv,
    rest_send, rest_recv, edge_send, edge_recv, face_sem,
):
    steps, tracers, levels, lat_rows, n_lat, n_lon, slots, capacity = dims
    merged = levels * lat_rows
    blocks = merged // LANES
    seg = LANES // SUB
    half = lat_rows // 2
    fields = tracers * levels
    my_lat, my_lon = lax.axis_index("lat"), lax.axis_index("lon")
    has_up = my_lat < n_lat - 1
    has_down = my_lat > 0

    def lon_peer(k):
        return (my_lat, lax.rem(my_lon + k, n_lon))

    def lat_peer(k):
        return (lax.rem(my_lat + k, n_lat), my_lon)

    def remote(src, dst, send, recv, device):
        return pltpu.make_async_remote_copy(
            src_ref=src, dst_ref=dst, send_sem=send, recv_sem=recv,
            device_id=device, device_id_type=MESH,
        )

    load_east = pltpu.make_async_copy(east_hbm, weight, local_sem.at[0])
    load_east.start()
    load_north = pltpu.make_async_copy(
        north_hbm, faces.at[:, :, pl.ds(PAD, lat_rows), :], local_sem.at[1]
    )
    load_north.start()

    gain_all[...] = jnp.zeros_like(gain_all)
    rest_all[...] = jnp.zeros_like(rest_all)
    face_in[...] = jnp.zeros_like(face_in)
    edge_in[...] = jnp.zeros_like(edge_in)
    barrier = pltpu.get_barrier_semaphore()
    for k in range(1, n_lon):
        pl.semaphore_signal(barrier, inc=1, device_id=lon_peer(k), device_id_type=MESH)
    for k in range(1, n_lat):
        pl.semaphore_signal(barrier, inc=1, device_id=lat_peer(k), device_id_type=MESH)

    owners = n_lat * n_lon
    spread = (
        lax.broadcasted_iota(jnp.int32, (owners, slots), 1) // capacity
        == lax.broadcasted_iota(jnp.int32, (owners, slots), 0)
    ).astype(F32)
    counts = jnp.dot(counts_ref[...].astype(F32), spread, preferred_element_type=F32)
    within = lax.rem(lax.broadcasted_iota(jnp.int32, (steps, slots), 1), capacity).astype(F32)
    live = (within < counts).astype(F32)
    features[...] = jnp.zeros_like(features)
    dep_row = steps * levels
    cell_row = dep_row + steps * tracers
    for n in range(steps):
        features[n * levels:(n + 1) * levels, :] = kern_ref[n]
        for t in range(tracers):
            at = dep_row + n * tracers + t
            features[at:at + 1, :] = dep_ref[n, t:t + 1, :] * live[n:n + 1, :]
        features[cell_row + n:cell_row + n + 1, :] = cells_ref[n:n + 1, :].astype(F32)
    by_slot = features[...].T
    for p in range(n_lat):
        for q in range(n_lon):
            at = (p * n_lon + q) * capacity
            sent[q, p] = by_slot[at:at + capacity]
    pl.semaphore_wait(barrier, n_lon - 1 + n_lat - 1)

    lon_copies = [
        remote(sent.at[lax.rem(my_lon + k, n_lon)], stage_lon.at[k],
               lon_send.at[k], lon_recv.at[k], lon_peer(k))
        for k in range(1, n_lon)
    ]
    for copy in lon_copies:
        copy.start()
    stage_lon[0] = sent[my_lon]

    load_north.wait()
    face_out[...] = faces[:, :, PAD + lat_rows - 1, :]
    up_device = (lax.rem(my_lat + 1, n_lat), my_lon)
    down_device = (lax.rem(my_lat + n_lat - 1, n_lat), my_lon)
    face_copy = remote(face_out, face_in, face_sem.at[0], face_sem.at[1], up_device)

    @pl.when(has_up)
    def _():
        face_copy.start()

    @pl.when(jnp.logical_not(has_up))
    def _():
        faces[:, :, PAD + lat_rows - 1, :] = jnp.zeros((steps, levels, LANES), F32)

    sub = lax.rem(lax.broadcasted_iota(jnp.int32, (blocks * SUB, LANES), 0), SUB)

    def ahead(x, d):
        return pltpu.roll(x, blocks * SUB - d, 0)

    def flat(x):
        return x.reshape(blocks * SUB, LANES)

    def gains(n):
        def one(b, carry):
            at = pl.ds(pl.multiple_of(b * LANES, LANES), LANES)
            east = weight[n, at, :]
            share = 1.0 / (1.0 + east)
            weight[n, at, :] = share
            gain_t[n, b] = (east * share).T
            return carry

        lax.fori_loop(0, blocks, one, 0, unroll=2)
        g = gain_t[n, :, pl.ds(seg - 1, SUB, stride=seg), :]
        for p in range(seg - 2, -1, -1):
            g = g * gain_t[n, :, pl.ds(p, SUB, stride=seg), :]
        g = flat(g)
        for level, d in enumerate((1, 2, 4)):
            gain_levels[n, level] = g
            g = jnp.where(sub < SUB - d, g * ahead(g, d), g)
        gain_levels[n, 3] = g
        for b in range(blocks):
            gain_all[0, n, b:b + 1, :] = g[b * SUB:b * SUB + 1, :]

    load_east.wait()
    gains(steps - 1)

    for copy in lon_copies:
        copy.wait()
    lat_copies = [
        remote(stage_lon.at[:, lax.rem(my_lat + k, n_lat)], stage_lat.at[k],
               lat_send.at[k], lat_recv.at[k], lat_peer(k))
        for k in range(1, n_lat)
    ]
    for copy in lat_copies:
        copy.start()
    stage_lat[0] = stage_lon[:, my_lat]
    for n in range(steps - 2, -1, -1):
        gains(n)
    gain_copies = [
        remote(gain_all.at[0], gain_all.at[k], gain_send.at[k], gain_recv.at[k], lon_peer(k))
        for k in range(1, n_lon)
    ]
    for copy in gain_copies:
        copy.start()
    for copy in lat_copies:
        copy.wait()

    got = stage_lat[...].reshape(slots, LANES)
    got_t[...] = got.T
    group = SUB
    shift = LANES.bit_length() - 1

    def split_cell(cell):
        row = lax.shift_right_logical(cell, shift)
        upper = (row >= half).astype(jnp.int32)
        return row - half * upper, (cell & (LANES - 1)) + LANES * upper

    def deposit(n, store):
        for t in range(tracers):
            at = dep_row + n * tracers + t
            term = got_t[at:at + 1, :] * got_t[n * levels:(n + 1) * levels, :]
            high = term.astype(BF16).astype(F32)
            term_hi[t * levels:(t + 1) * levels, :] = high
            term_lo[t * levels:(t + 1) * levels, :] = term - high
        lane_cell = got_t[cell_row + n:cell_row + n + 1, :].astype(jnp.int32)
        slot_row, _ = split_cell(lane_cell)
        _, slot_col = split_cell(stage_lat[...].reshape(slots, LANES)[
            :, cell_row + n:cell_row + n + 1].astype(jnp.int32))
        hot = (
            lax.broadcasted_iota(jnp.int32, (slots, 2 * LANES), 1) == slot_col
        ).astype(F32).astype(BF16)
        onehot[0:slots, :] = hot
        onehot[slots:2 * slots, :] = hot
        here = lax.broadcasted_iota(jnp.int32, (half, slots), 0) == slot_row

        def one(c, carry):
            for i in range(group):
                at = pl.ds(c * group + i, 1)
                part = pl.ds(i * half, half)
                left[part, 0:slots] = jnp.where(here, term_hi[at, :], 0.0).astype(BF16)
                left[part, slots:2 * slots] = jnp.where(here, term_lo[at, :], 0.0).astype(BF16)
            added = jnp.dot(left[...], onehot[...], preferred_element_type=F32)
            for i in range(group):
                block = added[i * half:(i + 1) * half]
                store(c * group + i, block[:, :LANES], block[:, LANES:])
            return carry

        lax.fori_loop(0, fields // group, one, 0)

    def into_field(i, low, high):
        field[i, PAD:PAD + half, :] = low
        field[i, PAD + half:PAD + lat_rows, :] = high

    def into_forcing(n):
        def store(i, low, high):
            forcing[n, i, 0:half, :] = low
            forcing[n, i, half:lat_rows, :] = high
        return store

    deposit(steps - 1, into_field)

    for n in range(steps - 1, -1, -1):
        edge_out[n, 0] = field[:, PAD, :]
        edge_out[n, 1] = field[:, PAD + lat_rows - 1, :]
        to_up = remote(edge_out.at[n, 1], edge_in.at[n, 0], edge_send.at[n, 1], edge_recv.at[n, 0], up_device)
        to_down = remote(edge_out.at[n, 0], edge_in.at[n, 1], edge_send.at[n, 0], edge_recv.at[n, 1], down_device)

        @pl.when(has_up)
        def _():
            to_up.start()

        @pl.when(has_down)
        def _():
            to_down.start()

        for t in range(tracers):
            surface = field[t * levels, PAD:PAD + lat_rows, :]
            if n == steps - 1:
                flux_ref[t] = surface
            else:
                flux_ref[t] = flux_ref[t] + surface
        if n == steps - 1:
            for m in range(steps - 2, -1, -1):
                deposit(m, into_forcing(m))

            @pl.when(has_down)
            def _():
                face_copy.wait_recv()

            @pl.when(has_up)
            def _():
                face_copy.wait_send()

            faces[:, :, PAD - 1, :] = face_in[...]

        @pl.when(has_up)
        def _():
            to_up.wait_send()
            to_down.wait_recv()

        @pl.when(has_down)
        def _():
            to_down.wait_send()
            to_up.wait_recv()

        field[:, PAD - 1, :] = edge_in[n, 0]
        field[:, PAD + lat_rows, :] = edge_in[n, 1]

        def lat_step(l, carry):
            northward = jnp.maximum(faces[n, l, PAD:PAD + lat_rows, :], 0.0)
            southward = jnp.minimum(faces[n, l, PAD - 1:PAD - 1 + lat_rows, :], 0.0)
            share = weight[n, pl.ds(pl.multiple_of(l * lat_rows, SUB), lat_rows), :]
            for t in range(tracers):
                i = t * levels + l
                a = field[i, PAD:PAD + lat_rows, :]
                above = field[i, PAD + 1:PAD + 1 + lat_rows, :]
                below = field[i, PAD - 1:PAD - 1 + lat_rows, :]
                y = a + northward * (above - a) + southward * (a - below)
                rows[pl.ds(pl.multiple_of(i * lat_rows, SUB), lat_rows), :] = share * y
            return carry

        lax.fori_loop(0, levels, lat_step, 0)

        def turn(b, carry):
            rows_t[b] = rows[pl.ds(pl.multiple_of(b * LANES, LANES), LANES), :].T
            return carry

        lax.fori_loop(0, tracers * blocks, turn, 0, unroll=4)

        def gain_at(p):
            return gain_t[n, :, pl.ds(p, SUB, stride=seg), :]

        def row_at(t, p):
            return (pl.ds(t * blocks, blocks), pl.ds(p, SUB, stride=seg), slice(None))

        rest = [rows_t[row_at(t, seg - 1)] for t in range(tracers)]
        for p in range(seg - 2, -1, -1):
            r = gain_at(p)
            rest = [r * s + rows_t[row_at(t, p)] for t, s in enumerate(rest)]
        rest = [flat(s) for s in rest]
        for level, d in enumerate((1, 2, 4)):
            g = gain_levels[n, level]
            rest = [jnp.where(sub < SUB - d, s + g * ahead(s, d), s) for s in rest]
        for t in range(tracers):
            for b in range(blocks):
                rest_all[n, 0, t, b:b + 1, :] = rest[t][b * SUB:b * SUB + 1, :]
        rest_copies = [
            remote(rest_all.at[n, 0], rest_all.at[n, k], rest_send.at[n, k], rest_recv.at[n, k], lon_peer(k))
            for k in range(1, n_lon)
        ]
        for copy in rest_copies:
            copy.start()
        if n == steps - 1:
            for copy in gain_copies:
                copy.wait()
        whole = gain_all[0, n]
        for k in range(1, n_lon):
            whole = whole * gain_all[k, n]
        for copy in rest_copies:
            copy.wait()
        ends = []
        for t in range(tracers):
            total = rest_all[n, 0, t]
            for k in range(1, n_lon):
                total = rest_all[n, k, t] + gain_all[k, n] * total
            closure = total / (1.0 - whole)
            wide = jnp.concatenate(
                [jnp.broadcast_to(closure[b:b + 1, :], (SUB, LANES)) for b in range(blocks)], 0
            )
            inclusive = gain_levels[n, 3] * wide + rest[t]
            end = jnp.where(sub == SUB - 1, wide, ahead(inclusive, 1))
            ends.append(end.reshape(blocks, SUB, LANES))
        for p in range(seg - 1, -1, -1):
            r = gain_at(p)
            for t in range(tracers):
                ends[t] = r * ends[t] + rows_t[row_at(t, p)]
                rows_t[row_at(t, p)] = ends[t]

        target = rows if n > 0 else out_ref

        def turn_back(b, carry):
            target[pl.ds(pl.multiple_of(b * LANES, LANES), LANES), :] = rows_t[b].T
            return carry

        lax.fori_loop(0, tracers * blocks, turn_back, 0, unroll=4)

        if n > 0:
            def add(i, carry):
                solved = rows[pl.ds(pl.multiple_of(i * lat_rows, SUB), lat_rows), :]
                field[i, PAD:PAD + lat_rows, :] = solved + forcing[n - 1, i]
                return carry

            lax.fori_loop(0, fields, add, 0, unroll=2)


def shards(east_courant, north_courant, kernels, departures, cells, counts):
    steps, levels, lat_rows, lon_cells = east_courant.shape
    tracers = departures.shape[1]
    n_lat, n_lon = lax.axis_size("lat"), lax.axis_size("lon")
    owners = n_lat * n_lon
    slots = cells.shape[1]
    capacity = slots // owners
    merged = levels * lat_rows
    blocks = merged // LANES
    padded = -(-blocks // SUB) * SUB
    fields = tracers * levels
    dims = (steps, tracers, levels, lat_rows, n_lat, n_lon, slots, capacity)
    vmem = pltpu.VMEM
    dma = pltpu.SemaphoreType.DMA
    whole = pl.BlockSpec(memory_space=pltpu.VMEM)
    anywhere = pl.BlockSpec(memory_space=pl.ANY)
    state, flux = pl.pallas_call(
        functools.partial(kernel, dims),
        out_shape=(
            jax.ShapeDtypeStruct((tracers * merged, lon_cells), F32),
            jax.ShapeDtypeStruct((tracers, lat_rows, lon_cells), F32),
        ),
        in_specs=[anywhere, anywhere, whole, whole, whole, whole],
        out_specs=(whole, whole),
        scratch_shapes=[
            vmem((steps, merged, LANES), F32),
            vmem((steps, levels, lat_rows + PAD, LANES), F32),
            vmem((steps, blocks, LANES, LANES), F32),
            vmem((steps, 4, blocks * SUB, LANES), F32),
            vmem((fields, lat_rows + 2 * PAD, LANES), F32),
            vmem((tracers * merged, LANES), F32),
            vmem((tracers * blocks, LANES, LANES), F32),
            vmem((max(steps - 1, 1), fields, lat_rows, LANES), F32),
            vmem((LANES, slots), F32),
            vmem((n_lon, n_lat, capacity, LANES), F32),
            vmem((n_lon, n_lat, capacity, LANES), F32),
            vmem((n_lat, n_lon, capacity, LANES), F32),
            vmem((LANES, slots), F32),
            vmem((fields, slots), F32),
            vmem((fields, slots), F32),
            vmem((SUB * lat_rows // 2, 2 * slots), BF16),
            vmem((2 * slots, 2 * LANES), BF16),
            vmem((steps, 2, fields, LANES), F32),
            vmem((steps, 2, fields, LANES), F32),
            vmem((steps, levels, LANES), F32),
            vmem((steps, levels, LANES), F32),
            vmem((n_lon, steps, padded, LANES), F32),
            vmem((steps, n_lon, tracers, padded, LANES), F32),
            dma((2,)),
            dma((n_lon,)), dma((n_lon,)),
            dma((n_lat,)), dma((n_lat,)),
            dma((n_lon,)), dma((n_lon,)),
            dma((steps, n_lon)), dma((steps, n_lon)),
            dma((steps, 2)), dma((steps, 2)),
            dma((2,)),
        ],
        compiler_params=pltpu.CompilerParams(
            collective_id=0, has_side_effects=True, vmem_limit_bytes=48 * 1024 * 1024
        ),
        name="adjoint_window",
    )(
        east_courant.reshape(steps, merged, lon_cells), north_courant,
        kernels, departures, cells, counts,
    )
    return state.reshape(tracers, levels, lat_rows, lon_cells), flux


def solution(mesh):
    return jax.shard_map(
        shards,
        mesh=mesh,
        in_specs=(
            P(None, None, "lat", "lon"),
            P(None, None, "lat", "lon"),
            P(None, None, ("lat", "lon")),
            P(None, None, ("lat", "lon")),
            P(None, ("lat", "lon")),
            P(None, ("lat", "lon")),
        ),
        out_specs=(P(None, None, "lat", "lon"), P(None, "lat", "lon")),
        check_vma=False,
    )
```

```python
import functools

import jax
import jax.numpy as jnp
from jax import lax
from jax.experimental import pallas as pl
from jax.experimental.pallas import tpu as pltpu
from jax.sharding import PartitionSpec as P

MESH = pl.DeviceIdType.MESH
SUB = 8
LANES = 128
PAD = 8
F32 = jnp.float32
BF16 = jnp.bfloat16


def kernel(
    dims,
    east_hbm, north_hbm, kern_hbm, dep_hbm, cells_hbm, counts_hbm,
    out_hbm, flux_hbm,
    flux_ref,
    kern_ref, dep_ref, cells_ref, counts_ref, edge_gain,
    weight, faces, gain_t, gain_levels, field, rows, rows_t, forcing,
    features, sent, stage_lon, stage_lat, got_t, term_hi, term_lo, left, onehot,
    edge_out, edge_in, face_out, face_in, gain_all, rest_all,
    local_sem, lon_send, lon_recv, lat_send, lat_recv, gain_send, gain_recv,
    rest_send, rest_recv, edge_send, edge_recv, face_sem,
):
    steps, tracers, levels, lat_rows, n_lat, n_lon, slots, capacity = dims
    merged = levels * lat_rows
    blocks = merged // LANES
    seg = LANES // SUB
    half = lat_rows // 2
    fields = tracers * levels
    my_lat, my_lon = lax.axis_index("lat"), lax.axis_index("lon")
    has_up = my_lat < n_lat - 1
    has_down = my_lat > 0

    def lon_peer(k):
        return (my_lat, lax.rem(my_lon + k, n_lon))

    def lat_peer(k):
        return (lax.rem(my_lat + k, n_lat), my_lon)

    def remote(src, dst, send, recv, device):
        return pltpu.make_async_remote_copy(
            src_ref=src, dst_ref=dst, send_sem=send, recv_sem=recv,
            device_id=device, device_id_type=MESH,
        )

    small = [
        pltpu.make_async_copy(src, dst, local_sem.at[2 + i])
        for i, (src, dst) in enumerate((
            (kern_hbm, kern_ref), (dep_hbm, dep_ref), (cells_hbm, cells_ref), (counts_hbm, counts_ref),
        ))
    ]
    for copy in small:
        copy.start()
    load_east = pltpu.make_async_copy(east_hbm, weight, local_sem.at[0])
    load_east.start()
    load_north = pltpu.make_async_copy(
        north_hbm, faces.at[:, :, pl.ds(PAD, lat_rows), :], local_sem.at[1]
    )
    load_north.start()

    gain_all[...] = jnp.zeros_like(gain_all)
    rest_all[...] = jnp.zeros_like(rest_all)
    face_in[...] = jnp.zeros_like(face_in)
    edge_in[...] = jnp.zeros_like(edge_in)
    field[:, PAD - 1, :] = jnp.zeros((fields, LANES), F32)
    field[:, PAD + lat_rows, :] = jnp.zeros((fields, LANES), F32)
    barrier = pltpu.get_barrier_semaphore()
    for k in range(1, n_lon):
        pl.semaphore_signal(barrier, inc=1, device_id=lon_peer(k), device_id_type=MESH)
    for k in range(1, n_lat):
        pl.semaphore_signal(barrier, inc=1, device_id=lat_peer(k), device_id_type=MESH)

    for copy in small:
        copy.wait()
    owners = n_lat * n_lon
    spread = (
        lax.broadcasted_iota(jnp.int32, (owners, slots), 1) // capacity
        == lax.broadcasted_iota(jnp.int32, (owners, slots), 0)
    ).astype(F32)
    counts = jnp.dot(counts_ref[...].astype(F32), spread, preferred_element_type=F32)
    within = lax.rem(lax.broadcasted_iota(jnp.int32, (steps, slots), 1), capacity).astype(F32)
    live = (within < counts).astype(F32)
    features[...] = jnp.zeros_like(features)
    dep_row = steps * levels
    cell_row = dep_row + steps * tracers
    for n in range(steps):
        features[n * levels:(n + 1) * levels, :] = kern_ref[n]
        for t in range(tracers):
            at = dep_row + n * tracers + t
            features[at:at + 1, :] = dep_ref[n, t:t + 1, :] * live[n:n + 1, :]
        features[cell_row + n:cell_row + n + 1, :] = cells_ref[n:n + 1, :].astype(F32)
    by_slot = features[...].T
    for p in range(n_lat):
        for q in range(n_lon):
            at = (p * n_lon + q) * capacity
            sent[q, p] = by_slot[at:at + capacity]
    pl.semaphore_wait(barrier, n_lon - 1 + n_lat - 1)

    lon_copies = [
        remote(sent.at[lax.rem(my_lon + k, n_lon)], stage_lon.at[k],
               lon_send.at[k], lon_recv.at[k], lon_peer(k))
        for k in range(1, n_lon)
    ]
    for copy in lon_copies:
        copy.start()
    stage_lon[0] = sent[my_lon]

    load_north.wait()
    face_out[...] = faces[:, :, PAD + lat_rows - 1, :]
    up_device = (lax.rem(my_lat + 1, n_lat), my_lon)
    down_device = (lax.rem(my_lat + n_lat - 1, n_lat), my_lon)
    face_copy = remote(face_out, face_in, face_sem.at[0], face_sem.at[1], up_device)

    @pl.when(has_up)
    def _():
        face_copy.start()

    @pl.when(jnp.logical_not(has_up))
    def _():
        faces[:, :, PAD + lat_rows - 1, :] = jnp.zeros((steps, levels, LANES), F32)

    sub = lax.rem(lax.broadcasted_iota(jnp.int32, (blocks * SUB, LANES), 0), SUB)

    def ahead(x, d):
        return pltpu.roll(x, blocks * SUB - d, 0)

    def flat(x):
        return x.reshape(blocks * SUB, LANES)

    def gains(n):
        def one(b, carry):
            at = pl.ds(pl.multiple_of(b * LANES, LANES), LANES)
            east = weight[n, at, :]
            share = 1.0 / (1.0 + east)
            weight[n, at, :] = share
            gain_t[n, b] = (east * share).T
            return carry

        lax.fori_loop(0, blocks, one, 0, unroll=2)
        g = gain_t[n, :, pl.ds(seg - 1, SUB, stride=seg), :]
        for p in range(seg - 2, -1, -1):
            g = g * gain_t[n, :, pl.ds(p, SUB, stride=seg), :]
        g = flat(g)
        for level, d in enumerate((1, 2, 4)):
            gain_levels[n, level] = g
            g = jnp.where(sub < SUB - d, g * ahead(g, d), g)
        gain_levels[n, 3] = g
        for b in range(blocks):
            gain_all[0, n, b:b + 1, :] = g[b * SUB:b * SUB + 1, :]

    load_east.wait()
    gains(steps - 1)

    for copy in lon_copies:
        copy.wait()
    lat_copies = [
        remote(stage_lon.at[:, lax.rem(my_lat + k, n_lat)], stage_lat.at[k],
               lat_send.at[k], lat_recv.at[k], lat_peer(k))
        for k in range(1, n_lat)
    ]
    for copy in lat_copies:
        copy.start()
    stage_lat[0] = stage_lon[:, my_lat]
    for n in range(steps - 2, -1, -1):
        gains(n)
    gain_copies = [
        remote(gain_all.at[0], gain_all.at[k], gain_send.at[k], gain_recv.at[k], lon_peer(k))
        for k in range(1, n_lon)
    ]
    for copy in gain_copies:
        copy.start()
    for copy in lat_copies:
        copy.wait()

    got = stage_lat[...].reshape(slots, LANES)
    got_t[...] = got.T
    group = SUB
    shift = LANES.bit_length() - 1

    def split_cell(cell):
        row = lax.shift_right_logical(cell, shift)
        upper = (row >= half).astype(jnp.int32)
        return row - half * upper, (cell & (LANES - 1)) + LANES * upper

    def deposit(n, store):
        for t in range(tracers):
            at = dep_row + n * tracers + t
            term = got_t[at:at + 1, :] * got_t[n * levels:(n + 1) * levels, :]
            high = term.astype(BF16).astype(F32)
            term_hi[t * levels:(t + 1) * levels, :] = high
            term_lo[t * levels:(t + 1) * levels, :] = term - high
        lane_cell = got_t[cell_row + n:cell_row + n + 1, :].astype(jnp.int32)
        slot_row, _ = split_cell(lane_cell)
        _, slot_col = split_cell(stage_lat[...].reshape(slots, LANES)[
            :, cell_row + n:cell_row + n + 1].astype(jnp.int32))
        hot = (
            lax.broadcasted_iota(jnp.int32, (slots, 2 * LANES), 1) == slot_col
        ).astype(F32).astype(BF16)
        onehot[0:slots, :] = hot
        onehot[slots:2 * slots, :] = hot
        here = lax.broadcasted_iota(jnp.int32, (half, slots), 0) == slot_row

        def one(c, carry):
            for i in range(group):
                at = pl.ds(c * group + i, 1)
                part = pl.ds(i * half, half)
                left[part, 0:slots] = jnp.where(here, term_hi[at, :], 0.0).astype(BF16)
                left[part, slots:2 * slots] = jnp.where(here, term_lo[at, :], 0.0).astype(BF16)
            added = jnp.dot(left[...], onehot[...], preferred_element_type=F32)
            for i in range(group):
                block = added[i * half:(i + 1) * half]
                store(c * group + i, block[:, :LANES], block[:, LANES:])
            return carry

        lax.fori_loop(0, fields // group, one, 0)

    def into_field(i, low, high):
        field[i, PAD:PAD + half, :] = low
        field[i, PAD + half:PAD + lat_rows, :] = high

    def into_forcing(n):
        def store(i, low, high):
            forcing[n, i, 0:half, :] = low
            forcing[n, i, half:lat_rows, :] = high
        return store

    deposit(steps - 1, into_field)

    def edge_copies(n, t):
        to_up = remote(edge_out.at[n, 1, t], edge_in.at[n, 0, t],
                       edge_send.at[n, 1, t], edge_recv.at[n, 0, t], up_device)
        to_down = remote(edge_out.at[n, 0, t], edge_in.at[n, 1, t],
                         edge_send.at[n, 0, t], edge_recv.at[n, 1, t], down_device)
        return to_up, to_down

    def send_edges(n, t):
        to_up, to_down = edge_copies(n, t)

        @pl.when(has_up)
        def _():
            to_up.start()

        @pl.when(has_down)
        def _():
            to_down.start()

    def wait_edges(n, t):
        to_up, to_down = edge_copies(n, t)

        @pl.when(has_up)
        def _():
            to_up.wait_send()
            to_down.wait_recv()

        @pl.when(has_down)
        def _():
            to_down.wait_send()
            to_up.wait_recv()

    def rest_copies(n, t):
        return [
            remote(rest_all.at[n, t, 0], rest_all.at[n, t, k],
                   rest_send.at[n, t, k], rest_recv.at[n, t, k], lon_peer(k))
            for k in range(1, n_lon)
        ]

    def bottom_rows(t, row):
        return (pl.ds(t * merged + row, levels, stride=lat_rows), slice(None))

    def add_flux(n, t):
        surface = field[t * levels, PAD:PAD + lat_rows, :]
        flux_ref[t] = surface if n == steps - 1 else flux_ref[t] + surface

    def lat_stencil(n, t):
        def one(l, carry):
            northward = jnp.maximum(faces[n, l, PAD:PAD + lat_rows, :], 0.0)
            southward = jnp.minimum(faces[n, l, PAD - 1:PAD - 1 + lat_rows, :], 0.0)
            share = weight[n, pl.ds(pl.multiple_of(l * lat_rows, SUB), lat_rows), :]
            i = t * levels + l
            a = field[i, PAD:PAD + lat_rows, :]
            above = field[i, PAD + 1:PAD + 1 + lat_rows, :]
            below = field[i, PAD - 1:PAD - 1 + lat_rows, :]
            y = a + northward * (above - a) + southward * (a - below)
            rows[pl.ds(pl.multiple_of(i * lat_rows, SUB), lat_rows), :] = share * y
            return carry

        lax.fori_loop(0, levels, one, 0, unroll=2)

    def gain_at(n, p):
        return gain_t[n, :, pl.ds(p, SUB, stride=seg), :]

    def row_at(t, p):
        return (pl.ds(t * blocks, blocks), pl.ds(p, SUB, stride=seg), slice(None))

    def block_rest(n, t):
        for side, row in ((0, 0), (1, lat_rows - 1)):
            at = bottom_rows(t, row)
            rows[at] = rows[at] + edge_gain[n, side] * edge_in[n, side, t]

        def turn(b, carry):
            b = b + t * blocks
            rows_t[b] = rows[pl.ds(pl.multiple_of(b * LANES, LANES), LANES), :].T
            return carry

        lax.fori_loop(0, blocks, turn, 0, unroll=4)
        rest = rows_t[row_at(t, seg - 1)]
        for p in range(seg - 2, -1, -1):
            rest = gain_at(n, p) * rest + rows_t[row_at(t, p)]
        rest = flat(rest)
        for level, d in enumerate((1, 2, 4)):
            rest = jnp.where(sub < SUB - d, rest + gain_levels[n, level] * ahead(rest, d), rest)
        for b in range(blocks):
            rest_all[n, t, 0, b:b + 1, :] = rest[b * SUB:b * SUB + 1, :]
        for copy in rest_copies(n, t):
            copy.start()
        return rest

    def finish(n, t, rest, scale):
        for copy in rest_copies(n, t):
            copy.wait()
        total = rest_all[n, t, 0]
        for k in range(1, n_lon):
            total = rest_all[n, t, k] + gain_all[k, n] * total
        closure = total * scale
        wide = jnp.concatenate(
            [jnp.broadcast_to(closure[b:b + 1, :], (SUB, LANES)) for b in range(blocks)], 0
        )
        inclusive = gain_levels[n, 3] * wide + rest
        end = jnp.where(sub == SUB - 1, wide, ahead(inclusive, 1)).reshape(blocks, SUB, LANES)
        for p in range(seg - 1, -1, -1):
            end = gain_at(n, p) * end + rows_t[row_at(t, p)]
            rows_t[row_at(t, p)] = end

        def turn_back(b, carry):
            b = b + t * blocks
            rows[pl.ds(pl.multiple_of(b * LANES, LANES), LANES), :] = rows_t[b].T
            return carry

        lax.fori_loop(0, blocks, turn_back, 0, unroll=4)

    def next_field(n, t):
        some = slice(t * levels, (t + 1) * levels)
        for side, row in ((0, 0), (1, lat_rows - 1)):
            edge_out[n, side, t] = rows[bottom_rows(t, row)] + forcing[n, some, row, :]
        send_edges(n, t)

        def add(l, carry):
            i = t * levels + l
            solved = rows[pl.ds(pl.multiple_of(i * lat_rows, SUB), lat_rows), :]
            field[i, PAD:PAD + lat_rows, :] = solved + forcing[n, i]
            return carry

        lax.fori_loop(0, levels, add, 0, unroll=2)
        add_flux(n, t)
        lat_stencil(n, t)

    def result_copy(t):
        some = pl.ds(t * merged, merged)
        return pltpu.make_async_copy(rows.at[some], out_hbm.at[some], local_sem.at[6 + t])

    flux_copy = pltpu.make_async_copy(flux_ref, flux_hbm, local_sem.at[6 + tracers])
    last = steps - 1
    for t in range(tracers):
        some = slice(t * levels, (t + 1) * levels)
        edge_out[last, 0, t] = field[some, PAD, :]
        edge_out[last, 1, t] = field[some, PAD + lat_rows - 1, :]
        send_edges(last, t)
    for m in range(steps - 2, -1, -1):
        deposit(m, into_forcing(m))

    @pl.when(has_down)
    def _():
        face_copy.wait_recv()

    @pl.when(has_up)
    def _():
        face_copy.wait_send()

    faces[:, :, PAD - 1, :] = face_in[...]
    for n in range(steps):
        low = weight[n, pl.ds(0, levels, stride=lat_rows), :]
        high = weight[n, pl.ds(lat_rows - 1, levels, stride=lat_rows), :]
        edge_gain[n, 0] = -jnp.minimum(face_in[n], 0.0) * low
        edge_gain[n, 1] = jnp.maximum(faces[n, :, PAD + lat_rows - 1, :], 0.0) * high
    for t in range(tracers):
        add_flux(last, t)
        lat_stencil(last, t)

    for n in range(last, -1, -1):
        rests = []
        for t in range(tracers):
            wait_edges(n, t)
            rests.append(block_rest(n, t))
        if n == 0:
            flux_copy.start()
        if n == last:
            for copy in gain_copies:
                copy.wait()
        whole = gain_all[0, n]
        for k in range(1, n_lon):
            whole = whole * gain_all[k, n]
        scale = 1.0 / (1.0 - whole)
        for t in range(tracers):
            finish(n, t, rests[t], scale)
            if n > 0:
                next_field(n - 1, t)
            else:
                result_copy(t).start()
    for t in range(tracers):
        result_copy(t).wait()
    flux_copy.wait()


def shards(east_courant, north_courant, kernels, departures, cells, counts):
    steps, levels, lat_rows, lon_cells = east_courant.shape
    tracers = departures.shape[1]
    n_lat, n_lon = lax.axis_size("lat"), lax.axis_size("lon")
    owners = n_lat * n_lon
    slots = cells.shape[1]
    capacity = slots // owners
    merged = levels * lat_rows
    blocks = merged // LANES
    padded = -(-blocks // SUB) * SUB
    fields = tracers * levels
    dims = (steps, tracers, levels, lat_rows, n_lat, n_lon, slots, capacity)
    vmem = pltpu.VMEM
    dma = pltpu.SemaphoreType.DMA
    far = pl.BlockSpec(memory_space=pltpu.HBM)
    state, flux = pl.pallas_call(
        functools.partial(kernel, dims),
        out_shape=(
            jax.ShapeDtypeStruct((tracers * merged, lon_cells), F32),
            jax.ShapeDtypeStruct((tracers, lat_rows, lon_cells), F32),
        ),
        in_specs=[far] * 6,
        out_specs=(far, far),
        scratch_shapes=[
            vmem((tracers, lat_rows, lon_cells), F32),
            vmem(kernels.shape, F32),
            vmem(departures.shape, F32),
            vmem(cells.shape, jnp.int32),
            vmem(counts.shape, jnp.int32),
            vmem((steps, 2, levels, LANES), F32),
            vmem((steps, merged, LANES), F32),
            vmem((steps, levels, lat_rows + PAD, LANES), F32),
            vmem((steps, blocks, LANES, LANES), F32),
            vmem((steps, 4, blocks * SUB, LANES), F32),
            vmem((fields, lat_rows + 2 * PAD, LANES), F32),
            vmem((tracers * merged, LANES), F32),
            vmem((tracers * blocks, LANES, LANES), F32),
            vmem((max(steps - 1, 1), fields, lat_rows, LANES), F32),
            vmem((LANES, slots), F32),
            vmem((n_lon, n_lat, capacity, LANES), F32),
            vmem((n_lon, n_lat, capacity, LANES), F32),
            vmem((n_lat, n_lon, capacity, LANES), F32),
            vmem((LANES, slots), F32),
            vmem((fields, slots), F32),
            vmem((fields, slots), F32),
            vmem((SUB * lat_rows // 2, 2 * slots), BF16),
            vmem((2 * slots, 2 * LANES), BF16),
            vmem((steps, 2, tracers, levels, LANES), F32),
            vmem((steps, 2, tracers, levels, LANES), F32),
            vmem((steps, levels, LANES), F32),
            vmem((steps, levels, LANES), F32),
            vmem((n_lon, steps, padded, LANES), F32),
            vmem((steps, tracers, n_lon, padded, LANES), F32),
            dma((7 + tracers,)),
            dma((n_lon,)), dma((n_lon,)),
            dma((n_lat,)), dma((n_lat,)),
            dma((n_lon,)), dma((n_lon,)),
            dma((steps, tracers, n_lon)), dma((steps, tracers, n_lon)),
            dma((steps, 2, tracers)), dma((steps, 2, tracers)),
            dma((2,)),
        ],
        compiler_params=pltpu.CompilerParams(
            collective_id=0, has_side_effects=True, vmem_limit_bytes=60 * 1024 * 1024
        ),
        name="adjoint_window",
    )(
        east_courant.reshape(steps, merged, lon_cells), north_courant,
        kernels, departures, cells, counts,
    )
    return state.reshape(tracers, levels, lat_rows, lon_cells), flux


def solution(mesh):
    return jax.shard_map(
        shards,
        mesh=mesh,
        in_specs=(
            P(None, None, "lat", "lon"),
            P(None, None, "lat", "lon"),
            P(None, None, ("lat", "lon")),
            P(None, None, ("lat", "lon")),
            P(None, ("lat", "lon")),
            P(None, ("lat", "lon")),
        ),
        out_specs=(P(None, None, "lat", "lon"), P(None, "lat", "lon")),
        check_vma=False,
    )
```

```python
import functools

import jax
import jax.numpy as jnp
from jax import lax
from jax.experimental import pallas as pl
from jax.experimental.pallas import tpu as pltpu
from jax.sharding import PartitionSpec as P

MESH = pl.DeviceIdType.MESH
SUB = 8
LANES = 128
PAD = 8
F32 = jnp.float32
BF16 = jnp.bfloat16


def kernel(
    dims,
    east_hbm, north_hbm, kern_hbm, dep_hbm, cells_hbm, counts_hbm,
    out_ref, flux_ref,
    kern_ref, dep_ref, cells_ref, counts_ref, edge_gain,
    weight, faces, turned, gain_seg, source_seg, gain_levels, field, rows, rows_t, forcing,
    features, sent, stage, got_t, term_hi, term_lo, left, onehot,
    edge_out, edge_in, face_out, face_in, gain_all, rest_all,
    local_sem, slot_sem, gain_send, gain_recv,
    rest_send, rest_recv, edge_send, edge_recv, face_sem,
):
    steps, tracers, levels, lat_rows, n_lat, n_lon, slots, capacity = dims
    merged = levels * lat_rows
    blocks = merged // LANES
    seg = LANES // SUB
    half = lat_rows // 2
    fields = tracers * levels
    my_lat, my_lon = lax.axis_index("lat"), lax.axis_index("lon")
    has_up = my_lat < n_lat - 1
    has_down = my_lat > 0

    lat_ids = [lax.rem(my_lat + i, n_lat) for i in range(n_lat)]
    lon_ids = [lax.rem(my_lon + j, n_lon) for j in range(n_lon)]
    offsets = [(i, j) for i in range(n_lat) for j in range(n_lon)][1:]

    def lon_peer(k):
        return (my_lat, lon_ids[k])

    def remote(src, dst, send, recv, device):
        return pltpu.make_async_remote_copy(
            src_ref=src, dst_ref=dst, send_sem=send, recv_sem=recv,
            device_id=device, device_id_type=MESH,
        )

    small = [
        pltpu.make_async_copy(src, dst, local_sem.at[2 + i])
        for i, (src, dst) in enumerate((
            (kern_hbm, kern_ref), (dep_hbm, dep_ref), (cells_hbm, cells_ref), (counts_hbm, counts_ref),
        ))
    ]
    for copy in small:
        copy.start()
    load_east = pltpu.make_async_copy(east_hbm, weight, local_sem.at[0])
    load_east.start()
    load_north = pltpu.make_async_copy(
        north_hbm, faces.at[:, :, pl.ds(PAD, lat_rows), :], local_sem.at[1]
    )
    load_north.start()

    gain_all[...] = jnp.zeros_like(gain_all)
    rest_all[...] = jnp.zeros_like(rest_all)
    face_in[...] = jnp.zeros_like(face_in)
    edge_in[...] = jnp.zeros_like(edge_in)
    field[:, PAD - 1, :] = jnp.zeros((fields, LANES), F32)
    field[:, PAD + lat_rows, :] = jnp.zeros((fields, LANES), F32)
    barrier = pltpu.get_barrier_semaphore()
    for i, j in offsets:
        pl.semaphore_signal(
            barrier, inc=1, device_id=(lat_ids[i], lon_ids[j]), device_id_type=MESH
        )

    for copy in small:
        copy.wait()
    owners = n_lat * n_lon
    spread = (
        lax.broadcasted_iota(jnp.int32, (owners, slots), 1) // capacity
        == lax.broadcasted_iota(jnp.int32, (owners, slots), 0)
    ).astype(F32)
    counts = jnp.dot(counts_ref[...].astype(F32), spread, preferred_element_type=F32)
    within = lax.rem(lax.broadcasted_iota(jnp.int32, (steps, slots), 1), capacity).astype(F32)
    live = (within < counts).astype(F32)
    features[...] = jnp.zeros_like(features)
    dep_row = steps * levels
    cell_row = dep_row + steps * tracers
    for n in range(steps):
        features[n * levels:(n + 1) * levels, :] = kern_ref[n]
        for t in range(tracers):
            at = dep_row + n * tracers + t
            features[at:at + 1, :] = dep_ref[n, t:t + 1, :] * live[n:n + 1, :]
        features[cell_row + n:cell_row + n + 1, :] = cells_ref[n:n + 1, :].astype(F32)
    sent[...] = features[...].T.reshape(sent.shape)
    pl.semaphore_wait(barrier, len(offsets))

    for i, j in offsets:
        remote(
            sent.at[lat_ids[i] * n_lon + lon_ids[j]], stage.at[i * n_lon + j],
            slot_sem.at[0], slot_sem.at[1], (lat_ids[i], lon_ids[j]),
        ).start()
    stage[0] = sent[my_lat * n_lon + my_lon]

    load_north.wait()
    face_out[...] = faces[:, :, PAD + lat_rows - 1, :]
    up_device = (lax.rem(my_lat + 1, n_lat), my_lon)
    down_device = (lax.rem(my_lat + n_lat - 1, n_lat), my_lon)
    face_copy = remote(face_out, face_in, face_sem.at[0], face_sem.at[1], up_device)

    @pl.when(has_up)
    def _():
        face_copy.start()

    @pl.when(jnp.logical_not(has_up))
    def _():
        faces[:, :, PAD + lat_rows - 1, :] = jnp.zeros((steps, levels, LANES), F32)

    sub = lax.rem(lax.broadcasted_iota(jnp.int32, (blocks * SUB, LANES), 0), SUB)

    def ahead(x, d):
        return pltpu.roll(x, blocks * SUB - d, 0)

    def flat(x):
        return x.reshape(blocks * SUB, LANES)

    def gains(n):
        def one(b, carry):
            at = pl.ds(pl.multiple_of(b * LANES, LANES), LANES)
            east = weight[n, at, :]
            share = 1.0 / (1.0 + east)
            weight[n, at, :] = share
            turned[b] = (east * share).T
            return carry

        lax.fori_loop(0, blocks, one, 0, unroll=2)
        g = None
        for p in range(seg - 1, -1, -1):
            part = flat(turned[:, pl.ds(p, SUB, stride=seg), :])
            gain_seg[n, p] = part
            g = part if g is None else g * part
        for level, d in enumerate((1, 2, 4)):
            gain_levels[n, level] = g
            g = jnp.where(sub < SUB - d, g * ahead(g, d), g)
        gain_levels[n, 3] = g
        for b in range(blocks):
            gain_all[0, n, b:b + 1, :] = g[b * SUB:b * SUB + 1, :]

    load_east.wait()
    gains(steps - 1)

    for n in range(steps - 2, -1, -1):
        gains(n)
    gain_copies = [
        remote(gain_all.at[0], gain_all.at[k], gain_send.at[k], gain_recv.at[k], lon_peer(k))
        for k in range(1, n_lon)
    ]
    for copy in gain_copies:
        copy.start()
    arrived = stage.at[pl.ds(1, owners - 1)]
    all_slots = remote(arrived, arrived, slot_sem.at[0], slot_sem.at[1], lon_peer(1))
    all_slots.wait_recv()
    got = stage[...].reshape(slots, LANES)
    got_t[...] = got.T
    group = SUB
    shift = LANES.bit_length() - 1

    def split_cell(cell):
        row = lax.shift_right_logical(cell, shift)
        upper = (row >= half).astype(jnp.int32)
        return row - half * upper, (cell & (LANES - 1)) + LANES * upper

    def deposit(n, store):
        for t in range(tracers):
            at = dep_row + n * tracers + t
            term = got_t[at:at + 1, :] * got_t[n * levels:(n + 1) * levels, :]
            high = term.astype(BF16).astype(F32)
            term_hi[t * levels:(t + 1) * levels, :] = high
            term_lo[t * levels:(t + 1) * levels, :] = term - high
        lane_cell = got_t[cell_row + n:cell_row + n + 1, :].astype(jnp.int32)
        slot_row, _ = split_cell(lane_cell)
        _, slot_col = split_cell(stage[...].reshape(slots, LANES)[
            :, cell_row + n:cell_row + n + 1].astype(jnp.int32))
        hot = (
            lax.broadcasted_iota(jnp.int32, (slots, 2 * LANES), 1) == slot_col
        ).astype(F32).astype(BF16)
        onehot[0:slots, :] = hot
        onehot[slots:2 * slots, :] = hot
        here = lax.broadcasted_iota(jnp.int32, (half, slots), 0) == slot_row

        def one(c, carry):
            for i in range(group):
                at = pl.ds(c * group + i, 1)
                part = pl.ds(i * half, half)
                left[part, 0:slots] = jnp.where(here, term_hi[at, :], 0.0).astype(BF16)
                left[part, slots:2 * slots] = jnp.where(here, term_lo[at, :], 0.0).astype(BF16)
            added = jnp.dot(left[...], onehot[...], preferred_element_type=F32)
            for i in range(group):
                block = added[i * half:(i + 1) * half]
                store(c * group + i, block[:, :LANES], block[:, LANES:])
            return carry

        lax.fori_loop(0, fields // group, one, 0)

    def into_field(i, low, high):
        field[i, PAD:PAD + half, :] = low
        field[i, PAD + half:PAD + lat_rows, :] = high

    def into_forcing(n):
        def store(i, low, high):
            forcing[n, i, 0:half, :] = low
            forcing[n, i, half:lat_rows, :] = high
        return store

    deposit(steps - 1, into_field)

    def edge_copies(n, t):
        to_up = remote(edge_out.at[n, 1, t], edge_in.at[n, 0, t],
                       edge_send.at[n, 1, t], edge_recv.at[n, 0, t], up_device)
        to_down = remote(edge_out.at[n, 0, t], edge_in.at[n, 1, t],
                         edge_send.at[n, 0, t], edge_recv.at[n, 1, t], down_device)
        return to_up, to_down

    def send_edges(n, t):
        to_up, to_down = edge_copies(n, t)

        @pl.when(has_up)
        def _():
            to_up.start()

        @pl.when(has_down)
        def _():
            to_down.start()

    def wait_edges(n, t):
        to_up, to_down = edge_copies(n, t)

        @pl.when(has_up)
        def _():
            to_up.wait_send()
            to_down.wait_recv()

        @pl.when(has_down)
        def _():
            to_down.wait_send()
            to_up.wait_recv()

    def rest_copies(n, t):
        return [
            remote(rest_all.at[n, t, 0], rest_all.at[n, t, k],
                   rest_send.at[n, t, k], rest_recv.at[n, t, k], lon_peer(k))
            for k in range(1, n_lon)
        ]

    def bottom_rows(t, row):
        return (pl.ds(t * merged + row, levels, stride=lat_rows), slice(None))

    def add_flux(n, t):
        surface = field[t * levels, PAD:PAD + lat_rows, :]
        flux_ref[t] = surface if n == steps - 1 else flux_ref[t] + surface

    def lat_stencil(n, t):
        def one(l, carry):
            northward = jnp.maximum(faces[n, l, PAD:PAD + lat_rows, :], 0.0)
            southward = jnp.minimum(faces[n, l, PAD - 1:PAD - 1 + lat_rows, :], 0.0)
            share = weight[n, pl.ds(pl.multiple_of(l * lat_rows, SUB), lat_rows), :]
            i = t * levels + l
            a = field[i, PAD:PAD + lat_rows, :]
            above = field[i, PAD + 1:PAD + 1 + lat_rows, :]
            below = field[i, PAD - 1:PAD - 1 + lat_rows, :]
            y = a + northward * (above - a) + southward * (a - below)
            rows[pl.ds(pl.multiple_of(i * lat_rows, SUB), lat_rows), :] = share * y
            return carry

        lax.fori_loop(0, levels, one, 0, unroll=2)

    def row_at(t, p):
        return (pl.ds(t * blocks, blocks), pl.ds(p, SUB, stride=seg), slice(None))

    def block_rest(n, t):
        for side, row in ((0, 0), (1, lat_rows - 1)):
            at = bottom_rows(t, row)
            rows[at] = rows[at] + edge_gain[n, side] * edge_in[n, side, t]

        def turn(b, carry):
            b = b + t * blocks
            rows_t[b] = rows[pl.ds(pl.multiple_of(b * LANES, LANES), LANES), :].T
            return carry

        lax.fori_loop(0, blocks, turn, 0, unroll=4)
        rest = None
        for p in range(seg - 1, -1, -1):
            part = flat(rows_t[row_at(t, p)])
            source_seg[t, p] = part
            rest = part if rest is None else gain_seg[n, p] * rest + part
        for level, d in enumerate((1, 2, 4)):
            rest = jnp.where(sub < SUB - d, rest + gain_levels[n, level] * ahead(rest, d), rest)
        for b in range(blocks):
            rest_all[n, t, 0, b:b + 1, :] = rest[b * SUB:b * SUB + 1, :]
        for copy in rest_copies(n, t):
            copy.start()
        return rest

    def finish(n, t, rest, scale):
        for copy in rest_copies(n, t):
            copy.wait()
        total = rest_all[n, t, 0]
        for k in range(1, n_lon):
            total = rest_all[n, t, k] + gain_all[k, n] * total
        closure = total * scale
        wide = jnp.concatenate(
            [jnp.broadcast_to(closure[b:b + 1, :], (SUB, LANES)) for b in range(blocks)], 0
        )
        inclusive = gain_levels[n, 3] * wide + rest
        end = jnp.where(sub == SUB - 1, wide, ahead(inclusive, 1))
        for p in range(seg - 1, -1, -1):
            end = gain_seg[n, p] * end + source_seg[t, p]
            rows_t[row_at(t, p)] = end.reshape(blocks, SUB, LANES)
        target = rows if n > 0 else out_ref

        def turn_back(b, carry):
            b = b + t * blocks
            target[pl.ds(pl.multiple_of(b * LANES, LANES), LANES), :] = rows_t[b].T
            return carry

        lax.fori_loop(0, blocks, turn_back, 0, unroll=4)

    def next_field(n, t):
        some = slice(t * levels, (t + 1) * levels)
        for side, row in ((0, 0), (1, lat_rows - 1)):
            edge_out[n, side, t] = rows[bottom_rows(t, row)] + forcing[n, some, row, :]
        send_edges(n, t)

        def add(l, carry):
            i = t * levels + l
            solved = rows[pl.ds(pl.multiple_of(i * lat_rows, SUB), lat_rows), :]
            field[i, PAD:PAD + lat_rows, :] = solved + forcing[n, i]
            return carry

        lax.fori_loop(0, levels, add, 0, unroll=2)
        add_flux(n, t)
        lat_stencil(n, t)

    last = steps - 1
    for t in range(tracers):
        some = slice(t * levels, (t + 1) * levels)
        edge_out[last, 0, t] = field[some, PAD, :]
        edge_out[last, 1, t] = field[some, PAD + lat_rows - 1, :]
        send_edges(last, t)
    for m in range(steps - 2, -1, -1):
        deposit(m, into_forcing(m))

    @pl.when(has_down)
    def _():
        face_copy.wait_recv()

    @pl.when(has_up)
    def _():
        face_copy.wait_send()

    faces[:, :, PAD - 1, :] = face_in[...]
    for n in range(steps):
        low = weight[n, pl.ds(0, levels, stride=lat_rows), :]
        high = weight[n, pl.ds(lat_rows - 1, levels, stride=lat_rows), :]
        edge_gain[n, 0] = -jnp.minimum(face_in[n], 0.0) * low
        edge_gain[n, 1] = jnp.maximum(faces[n, :, PAD + lat_rows - 1, :], 0.0) * high
    for t in range(tracers):
        add_flux(last, t)
        lat_stencil(last, t)

    for n in range(last, -1, -1):
        rests = []
        for t in range(tracers):
            wait_edges(n, t)
            rests.append(block_rest(n, t))
        if n == last:
            for copy in gain_copies:
                copy.wait()
        whole = gain_all[0, n]
        for k in range(1, n_lon):
            whole = whole * gain_all[k, n]
        scale = 1.0 / (1.0 - whole)
        for t in range(tracers):
            finish(n, t, rests[t], scale)
            if n > 0:
                next_field(n - 1, t)
    all_slots.wait_send()


def shards(east_courant, north_courant, kernels, departures, cells, counts):
    steps, levels, lat_rows, lon_cells = east_courant.shape
    tracers = departures.shape[1]
    n_lat, n_lon = lax.axis_size("lat"), lax.axis_size("lon")
    owners = n_lat * n_lon
    slots = cells.shape[1]
    capacity = slots // owners
    merged = levels * lat_rows
    blocks = merged // LANES
    padded = -(-blocks // SUB) * SUB
    fields = tracers * levels
    dims = (steps, tracers, levels, lat_rows, n_lat, n_lon, slots, capacity)
    vmem = pltpu.VMEM
    dma = pltpu.SemaphoreType.DMA
    near = pl.BlockSpec(memory_space=pltpu.VMEM)
    far = pl.BlockSpec(memory_space=pltpu.HBM)
    state, flux = pl.pallas_call(
        functools.partial(kernel, dims),
        out_shape=(
            vmem((tracers * merged, lon_cells), F32),
            vmem((tracers, lat_rows, lon_cells), F32),
        ),
        in_specs=[far] * 6,
        out_specs=(near, near),
        scratch_shapes=[
            vmem(kernels.shape, F32),
            vmem(departures.shape, F32),
            vmem(cells.shape, jnp.int32),
            vmem(counts.shape, jnp.int32),
            vmem((steps, 2, levels, LANES), F32),
            vmem((steps, merged, LANES), F32),
            vmem((steps, levels, lat_rows + PAD, LANES), F32),
            vmem((blocks, LANES, LANES), F32),
            vmem((steps, LANES // SUB, blocks * SUB, LANES), F32),
            vmem((tracers, LANES // SUB, blocks * SUB, LANES), F32),
            vmem((steps, 4, blocks * SUB, LANES), F32),
            vmem((fields, lat_rows + 2 * PAD, LANES), F32),
            vmem((tracers * merged, LANES), F32),
            vmem((tracers * blocks, LANES, LANES), F32),
            vmem((max(steps - 1, 1), fields, lat_rows, LANES), F32),
            vmem((LANES, slots), F32),
            vmem((owners, capacity, LANES), F32),
            vmem((owners, capacity, LANES), F32),
            vmem((LANES, slots), F32),
            vmem((fields, slots), F32),
            vmem((fields, slots), F32),
            vmem((SUB * lat_rows // 2, 2 * slots), BF16),
            vmem((2 * slots, 2 * LANES), BF16),
            vmem((steps, 2, tracers, levels, LANES), F32),
            vmem((steps, 2, tracers, levels, LANES), F32),
            vmem((steps, levels, LANES), F32),
            vmem((steps, levels, LANES), F32),
            vmem((n_lon, steps, padded, LANES), F32),
            vmem((steps, tracers, n_lon, padded, LANES), F32),
            dma((6,)),
            dma((2,)),
            dma((n_lon,)), dma((n_lon,)),
            dma((steps, tracers, n_lon)), dma((steps, tracers, n_lon)),
            dma((steps, 2, tracers)), dma((steps, 2, tracers)),
            dma((2,)),
        ],
        compiler_params=pltpu.CompilerParams(
            collective_id=0, has_side_effects=True, vmem_limit_bytes=40 * 1024 * 1024
        ),
        name="adjoint_window",
    )(
        *(
            pltpu.with_memory_space_constraint(x, pltpu.HBM)
            for x in (
                east_courant.reshape(steps, merged, lon_cells), north_courant,
                kernels, departures, cells, counts,
            )
        )
    )
    return state.reshape(tracers, levels, lat_rows, lon_cells), flux


def solution(mesh):
    return jax.shard_map(
        shards,
        mesh=mesh,
        in_specs=(
            P(None, None, "lat", "lon"),
            P(None, None, "lat", "lon"),
            P(None, None, ("lat", "lon")),
            P(None, None, ("lat", "lon")),
            P(None, ("lat", "lon")),
            P(None, ("lat", "lon")),
        ),
        out_specs=(P(None, None, "lat", "lon"), P(None, "lat", "lon")),
        check_vma=False,
    )
```

```python
import functools

import jax
import jax.numpy as jnp
from jax import lax
from jax.experimental import pallas as pl
from jax.experimental.pallas import tpu as pltpu
from jax.sharding import PartitionSpec as P

MESH = pl.DeviceIdType.MESH
SUB = 8
LANES = 128
PAD = 8
F32 = jnp.float32
BF16 = jnp.bfloat16


def kernel(
    dims,
    east_hbm, north_hbm, kern_hbm, dep_hbm, cells_hbm, counts_hbm,
    gain_seg, source_seg, end_ref, flux_ref,
    kern_ref, dep_ref, cells_ref, counts_ref, edge_gain,
    weight, faces, turned, gain_levels, field, rows, rows_t, forcing,
    features, sent, stage, got_t, term_hi, term_lo, left, onehot,
    edge_out, edge_in, face_out, face_in, gain_all, rest_all,
    local_sem, slot_sem, gain_send, gain_recv,
    rest_send, rest_recv, edge_send, edge_recv, face_sem,
):
    steps, tracers, levels, lat_rows, n_lat, n_lon, slots, capacity = dims
    merged = levels * lat_rows
    blocks = merged // LANES
    seg = LANES // SUB
    half = lat_rows // 2
    fields = tracers * levels
    my_lat, my_lon = lax.axis_index("lat"), lax.axis_index("lon")
    has_up = my_lat < n_lat - 1
    has_down = my_lat > 0

    lat_ids = [lax.rem(my_lat + i, n_lat) for i in range(n_lat)]
    lon_ids = [lax.rem(my_lon + j, n_lon) for j in range(n_lon)]
    offsets = [(i, j) for i in range(n_lat) for j in range(n_lon)][1:]

    def lon_peer(k):
        return (my_lat, lon_ids[k])

    def remote(src, dst, send, recv, device):
        return pltpu.make_async_remote_copy(
            src_ref=src, dst_ref=dst, send_sem=send, recv_sem=recv,
            device_id=device, device_id_type=MESH,
        )

    small = [
        pltpu.make_async_copy(src, dst, local_sem.at[2 + i])
        for i, (src, dst) in enumerate((
            (kern_hbm, kern_ref), (dep_hbm, dep_ref), (cells_hbm, cells_ref), (counts_hbm, counts_ref),
        ))
    ]
    for copy in small:
        copy.start()
    load_east = pltpu.make_async_copy(east_hbm, weight, local_sem.at[0])
    load_east.start()
    load_north = pltpu.make_async_copy(
        north_hbm, faces.at[:, :, pl.ds(PAD, lat_rows), :], local_sem.at[1]
    )
    load_north.start()

    gain_all[...] = jnp.zeros_like(gain_all)
    rest_all[...] = jnp.zeros_like(rest_all)
    face_in[...] = jnp.zeros_like(face_in)
    edge_in[...] = jnp.zeros_like(edge_in)
    field[:, PAD - 1, :] = jnp.zeros((fields, LANES), F32)
    field[:, PAD + lat_rows, :] = jnp.zeros((fields, LANES), F32)
    barrier = pltpu.get_barrier_semaphore()
    for i, j in offsets:
        pl.semaphore_signal(
            barrier, inc=1, device_id=(lat_ids[i], lon_ids[j]), device_id_type=MESH
        )

    for copy in small:
        copy.wait()
    owners = n_lat * n_lon
    spread = (
        lax.broadcasted_iota(jnp.int32, (owners, slots), 1) // capacity
        == lax.broadcasted_iota(jnp.int32, (owners, slots), 0)
    ).astype(F32)
    counts = jnp.dot(counts_ref[...].astype(F32), spread, preferred_element_type=F32)
    within = lax.rem(lax.broadcasted_iota(jnp.int32, (steps, slots), 1), capacity).astype(F32)
    live = (within < counts).astype(F32)
    features[...] = jnp.zeros_like(features)
    dep_row = steps * levels
    cell_row = dep_row + steps * tracers
    for n in range(steps):
        features[n * levels:(n + 1) * levels, :] = kern_ref[n]
        for t in range(tracers):
            at = dep_row + n * tracers + t
            features[at:at + 1, :] = dep_ref[n, t:t + 1, :] * live[n:n + 1, :]
        features[cell_row + n:cell_row + n + 1, :] = cells_ref[n:n + 1, :].astype(F32)
    sent[...] = features[...].T.reshape(sent.shape)
    pl.semaphore_wait(barrier, len(offsets))

    for i, j in offsets:
        remote(
            sent.at[lat_ids[i] * n_lon + lon_ids[j]], stage.at[i * n_lon + j],
            slot_sem.at[0], slot_sem.at[1], (lat_ids[i], lon_ids[j]),
        ).start()
    stage[0] = sent[my_lat * n_lon + my_lon]

    load_north.wait()
    face_out[...] = faces[:, :, PAD + lat_rows - 1, :]
    up_device = (lax.rem(my_lat + 1, n_lat), my_lon)
    down_device = (lax.rem(my_lat + n_lat - 1, n_lat), my_lon)
    face_copy = remote(face_out, face_in, face_sem.at[0], face_sem.at[1], up_device)

    @pl.when(has_up)
    def _():
        face_copy.start()

    @pl.when(jnp.logical_not(has_up))
    def _():
        faces[:, :, PAD + lat_rows - 1, :] = jnp.zeros((steps, levels, LANES), F32)

    sub = lax.rem(lax.broadcasted_iota(jnp.int32, (blocks * SUB, LANES), 0), SUB)

    def ahead(x, d):
        return pltpu.roll(x, blocks * SUB - d, 0)

    def flat(x):
        return x.reshape(blocks * SUB, LANES)

    def gains(n):
        def one(b, carry):
            at = pl.ds(pl.multiple_of(b * LANES, LANES), LANES)
            east = weight[n, at, :]
            share = 1.0 / (1.0 + east)
            weight[n, at, :] = share
            turned[b] = (east * share).T
            return carry

        lax.fori_loop(0, blocks, one, 0, unroll=4)
        g = None
        for p in range(seg - 1, -1, -1):
            part = flat(turned[:, pl.ds(p, SUB, stride=seg), :])
            gain_seg[n, p] = part
            g = part if g is None else g * part
        for level, d in enumerate((1, 2, 4)):
            gain_levels[n, level] = g
            g = jnp.where(sub < SUB - d, g * ahead(g, d), g)
        gain_levels[n, 3] = g
        for b in range(blocks):
            gain_all[n, 0, b:b + 1, :] = g[b * SUB:b * SUB + 1, :]

    load_east.wait()
    gains(steps - 1)

    def gain_copies(n):
        return [
            remote(gain_all.at[n, 0], gain_all.at[n, k], gain_send.at[n, k], gain_recv.at[n, k], lon_peer(k))
            for k in range(1, n_lon)
        ]

    for copy in gain_copies(steps - 1):
        copy.start()
    arrived = stage.at[pl.ds(1, owners - 1)]
    all_slots = remote(arrived, arrived, slot_sem.at[0], slot_sem.at[1], lon_peer(1))
    all_slots.wait_recv()
    got = stage[...].reshape(slots, LANES)
    got_t[...] = got.T
    group = SUB
    shift = LANES.bit_length() - 1

    def split_cell(cell):
        row = lax.shift_right_logical(cell, shift)
        upper = (row >= half).astype(jnp.int32)
        return row - half * upper, (cell & (LANES - 1)) + LANES * upper

    def deposit(n, store):
        for t in range(tracers):
            at = dep_row + n * tracers + t
            term = got_t[at:at + 1, :] * got_t[n * levels:(n + 1) * levels, :]
            high = term.astype(BF16).astype(F32)
            term_hi[t * levels:(t + 1) * levels, :] = high
            term_lo[t * levels:(t + 1) * levels, :] = term - high
        lane_cell = got_t[cell_row + n:cell_row + n + 1, :].astype(jnp.int32)
        slot_row, _ = split_cell(lane_cell)
        _, slot_col = split_cell(stage[...].reshape(slots, LANES)[
            :, cell_row + n:cell_row + n + 1].astype(jnp.int32))
        hot = (
            lax.broadcasted_iota(jnp.int32, (slots, 2 * LANES), 1) == slot_col
        ).astype(F32).astype(BF16)
        onehot[0:slots, :] = hot
        onehot[slots:2 * slots, :] = hot
        here = lax.broadcasted_iota(jnp.int32, (half, slots), 0) == slot_row

        for c in range(fields // group):
            for i in range(group):
                at = pl.ds(c * group + i, 1)
                part = pl.ds(i * half, half)
                left[c % 2, part, 0:slots] = jnp.where(here, term_hi[at, :], 0.0).astype(BF16)
                left[c % 2, part, slots:2 * slots] = jnp.where(here, term_lo[at, :], 0.0).astype(BF16)
            added = jnp.dot(left[c % 2], onehot[...], preferred_element_type=F32)
            for i in range(group):
                block = added[i * half:(i + 1) * half]
                store(c * group + i, block[:, :LANES], block[:, LANES:])

    def into_field(i, low, high):
        field[i, PAD:PAD + half, :] = low
        field[i, PAD + half:PAD + lat_rows, :] = high

    def into_forcing(n):
        def store(i, low, high):
            forcing[n, i, 0:half, :] = low
            forcing[n, i, half:lat_rows, :] = high
        return store

    deposit(steps - 1, into_field)

    def edge_copies(n, t):
        to_up = remote(edge_out.at[n, 1, t], edge_in.at[n, 0, t],
                       edge_send.at[n, 1, t], edge_recv.at[n, 0, t], up_device)
        to_down = remote(edge_out.at[n, 0, t], edge_in.at[n, 1, t],
                         edge_send.at[n, 0, t], edge_recv.at[n, 1, t], down_device)
        return to_up, to_down

    def send_edges(n, t):
        to_up, to_down = edge_copies(n, t)

        @pl.when(has_up)
        def _():
            to_up.start()

        @pl.when(has_down)
        def _():
            to_down.start()

    def wait_edges(n, t):
        to_up, to_down = edge_copies(n, t)

        @pl.when(has_up)
        def _():
            to_up.wait_send()
            to_down.wait_recv()

        @pl.when(has_down)
        def _():
            to_down.wait_send()
            to_up.wait_recv()

    def rest_copies(n, t):
        return [
            remote(rest_all.at[n, t, 0], rest_all.at[n, t, k],
                   rest_send.at[n, t, k], rest_recv.at[n, t, k], lon_peer(k))
            for k in range(1, n_lon)
        ]

    def bottom_rows(t, row):
        return (pl.ds(t * merged + row, levels, stride=lat_rows), slice(None))

    def add_flux(n, t):
        surface = field[t * levels, PAD:PAD + lat_rows, :]
        flux_ref[t] = surface if n == steps - 1 else flux_ref[t] + surface

    def lat_stencil(n, t):
        def one(l, carry):
            northward = jnp.maximum(faces[n, l, PAD:PAD + lat_rows, :], 0.0)
            southward = jnp.minimum(faces[n, l, PAD - 1:PAD - 1 + lat_rows, :], 0.0)
            share = weight[n, pl.ds(pl.multiple_of(l * lat_rows, SUB), lat_rows), :]
            i = t * levels + l
            a = field[i, PAD:PAD + lat_rows, :]
            above = field[i, PAD + 1:PAD + 1 + lat_rows, :]
            below = field[i, PAD - 1:PAD - 1 + lat_rows, :]
            y = a + northward * (above - a) + southward * (a - below)
            rows[pl.ds(pl.multiple_of(i * lat_rows, SUB), lat_rows), :] = share * y
            return carry

        lax.fori_loop(0, levels, one, 0, unroll=2)

    def row_at(t, p):
        return (pl.ds(t * blocks, blocks), pl.ds(p, SUB, stride=seg), slice(None))

    def block_rest(n, t):
        for side, row in ((0, 0), (1, lat_rows - 1)):
            at = bottom_rows(t, row)
            rows[at] = rows[at] + edge_gain[n, side] * edge_in[n, side, t]

        def turn(b, carry):
            b = b + t * blocks
            rows_t[b] = rows[pl.ds(pl.multiple_of(b * LANES, LANES), LANES), :].T
            return carry

        lax.fori_loop(0, blocks, turn, 0, unroll=True)
        rest = None
        for p in range(seg - 1, -1, -1):
            part = flat(rows_t[row_at(t, p)])
            source_seg[t, p] = part
            rest = part if rest is None else gain_seg[n, p] * rest + part
        for level, d in enumerate((1, 2, 4)):
            rest = jnp.where(sub < SUB - d, rest + gain_levels[n, level] * ahead(rest, d), rest)
        for b in range(blocks):
            rest_all[n, t, 0, b:b + 1, :] = rest[b * SUB:b * SUB + 1, :]
        for copy in rest_copies(n, t):
            copy.start()
        return rest

    def finish(n, t, rest, scale):
        for copy in rest_copies(n, t):
            copy.wait()
        total = rest_all[n, t, 0]
        for k in range(1, n_lon):
            total = rest_all[n, t, k] + gain_all[n, k] * total
        closure = total * scale
        wide = jnp.concatenate(
            [jnp.broadcast_to(closure[b:b + 1, :], (SUB, LANES)) for b in range(blocks)], 0
        )
        inclusive = gain_levels[n, 3] * wide + rest
        end = jnp.where(sub == SUB - 1, wide, ahead(inclusive, 1))
        if n == 0:
            end_ref[t] = end
            return
        for p in range(seg - 1, -1, -1):
            end = gain_seg[n, p] * end + source_seg[t, p]
            rows_t[row_at(t, p)] = end.reshape(blocks, SUB, LANES)

        def turn_back(b, carry):
            b = b + t * blocks
            rows[pl.ds(pl.multiple_of(b * LANES, LANES), LANES), :] = rows_t[b].T
            return carry

        lax.fori_loop(0, blocks, turn_back, 0, unroll=True)

    def next_field(n, t):
        some = slice(t * levels, (t + 1) * levels)
        for side, row in ((0, 0), (1, lat_rows - 1)):
            edge_out[n, side, t] = rows[bottom_rows(t, row)] + forcing[n, some, row, :]
        send_edges(n, t)

        def add(l, carry):
            i = t * levels + l
            solved = rows[pl.ds(pl.multiple_of(i * lat_rows, SUB), lat_rows), :]
            field[i, PAD:PAD + lat_rows, :] = solved + forcing[n, i]
            return carry

        lax.fori_loop(0, levels, add, 0, unroll=2)
        add_flux(n, t)
        lat_stencil(n, t)

    last = steps - 1
    for t in range(tracers):
        some = slice(t * levels, (t + 1) * levels)
        edge_out[last, 0, t] = field[some, PAD, :]
        edge_out[last, 1, t] = field[some, PAD + lat_rows - 1, :]
        send_edges(last, t)
    for m in range(steps - 2, -1, -1):
        gains(m)
        for copy in gain_copies(m):
            copy.start()

    @pl.when(has_down)
    def _():
        face_copy.wait_recv()

    @pl.when(has_up)
    def _():
        face_copy.wait_send()

    faces[:, :, PAD - 1, :] = face_in[...]
    for n in range(steps):
        low = weight[n, pl.ds(0, levels, stride=lat_rows), :]
        high = weight[n, pl.ds(lat_rows - 1, levels, stride=lat_rows), :]
        edge_gain[n, 0] = -jnp.minimum(face_in[n], 0.0) * low
        edge_gain[n, 1] = jnp.maximum(faces[n, :, PAD + lat_rows - 1, :], 0.0) * high
    for t in range(tracers):
        add_flux(last, t)
        lat_stencil(last, t)

    for n in range(last, -1, -1):
        rests = []
        for t in range(tracers):
            wait_edges(n, t)
            rests.append(block_rest(n, t))
        if n == last:
            for m in range(steps - 2, -1, -1):
                deposit(m, into_forcing(m))
        for copy in gain_copies(n):
            copy.wait()
        whole = gain_all[n, 0]
        for k in range(1, n_lon):
            whole = whole * gain_all[n, k]
        scale = 1.0 / (1.0 - whole)
        for t in range(tracers):
            finish(n, t, rests[t], scale)
            if n > 0:
                next_field(n - 1, t)
    all_slots.wait_send()


def closing(
    dims, gain_seg, source_seg, end_ref, flux_ref, out_hbm, flux_hbm, rows_t, rows, sems
):
    tracers, blocks, group = dims
    seg = LANES // SUB
    flux_copy = pltpu.make_async_copy(flux_ref, flux_hbm, sems.at[0])
    flux_copy.start()
    copies = [flux_copy]
    for t in range(tracers):
        end = end_ref[t]
        for p in range(seg - 1, -1, -1):
            end = gain_seg[0, p] * end + source_seg[t, p]
            rows_t[t, :, pl.ds(p, SUB, stride=seg), :] = end.reshape(blocks, SUB, LANES)
        for first in range(0, blocks, group):
            for b in range(first, first + group):
                at = (t * blocks + b) * LANES
                rows[at:at + LANES, :] = rows_t[t, b].T
            some = pl.ds((t * blocks + first) * LANES, group * LANES)
            copies.append(pltpu.make_async_copy(rows.at[some], out_hbm.at[some], sems.at[len(copies)]))
            copies[-1].start()
    for copy in copies:
        copy.wait()


def shards(east_courant, north_courant, kernels, departures, cells, counts):
    steps, levels, lat_rows, lon_cells = east_courant.shape
    tracers = departures.shape[1]
    n_lat, n_lon = lax.axis_size("lat"), lax.axis_size("lon")
    owners = n_lat * n_lon
    slots = cells.shape[1]
    capacity = slots // owners
    merged = levels * lat_rows
    blocks = merged // LANES
    padded = -(-blocks // SUB) * SUB
    fields = tracers * levels
    dims = (steps, tracers, levels, lat_rows, n_lat, n_lon, slots, capacity)
    vmem = pltpu.VMEM
    dma = pltpu.SemaphoreType.DMA
    near = pl.BlockSpec(memory_space=pltpu.VMEM)
    far = pl.BlockSpec(memory_space=pltpu.HBM)
    seg = LANES // SUB
    parts = pl.pallas_call(
        functools.partial(kernel, dims),
        out_shape=(
            vmem((steps, seg, blocks * SUB, LANES), F32),
            vmem((tracers, seg, blocks * SUB, LANES), F32),
            vmem((tracers, blocks * SUB, LANES), F32),
            vmem((tracers, lat_rows, lon_cells), F32),
        ),
        in_specs=[far] * 6,
        out_specs=(near,) * 4,
        scratch_shapes=[
            vmem(kernels.shape, F32),
            vmem(departures.shape, F32),
            vmem(cells.shape, jnp.int32),
            vmem(counts.shape, jnp.int32),
            vmem((steps, 2, levels, LANES), F32),
            vmem((steps, merged, LANES), F32),
            vmem((steps, levels, lat_rows + PAD, LANES), F32),
            vmem((blocks, LANES, LANES), F32),
            vmem((steps, 4, blocks * SUB, LANES), F32),
            vmem((fields, lat_rows + 2 * PAD, LANES), F32),
            vmem((tracers * merged, LANES), F32),
            vmem((tracers * blocks, LANES, LANES), F32),
            vmem((max(steps - 1, 1), fields, lat_rows, LANES), F32),
            vmem((LANES, slots), F32),
            vmem((owners, capacity, LANES), F32),
            vmem((owners, capacity, LANES), F32),
            vmem((LANES, slots), F32),
            vmem((fields, slots), F32),
            vmem((fields, slots), F32),
            vmem((2, SUB * lat_rows // 2, 2 * slots), BF16),
            vmem((2 * slots, 2 * LANES), BF16),
            vmem((steps, 2, tracers, levels, LANES), F32),
            vmem((steps, 2, tracers, levels, LANES), F32),
            vmem((steps, levels, LANES), F32),
            vmem((steps, levels, LANES), F32),
            vmem((steps, n_lon, padded, LANES), F32),
            vmem((steps, tracers, n_lon, padded, LANES), F32),
            dma((6,)),
            dma((2,)),
            dma((steps, n_lon)), dma((steps, n_lon)),
            dma((steps, tracers, n_lon)), dma((steps, tracers, n_lon)),
            dma((steps, 2, tracers)), dma((steps, 2, tracers)),
            dma((2,)),
        ],
        compiler_params=pltpu.CompilerParams(
            collective_id=0, has_side_effects=True, vmem_limit_bytes=40 * 1024 * 1024
        ),
        name="adjoint_window",
    )(
        *(
            pltpu.with_memory_space_constraint(x, pltpu.HBM)
            for x in (
                east_courant.reshape(steps, merged, lon_cells), north_courant,
                kernels, departures, cells, counts,
            )
        )
    )
    group = 4 if blocks % 4 == 0 else 1
    state, flux = pl.pallas_call(
        functools.partial(closing, (tracers, blocks, group)),
        out_shape=(
            jax.ShapeDtypeStruct((tracers * merged, lon_cells), F32),
            jax.ShapeDtypeStruct((tracers, lat_rows, lon_cells), F32),
        ),
        in_specs=[near] * 4,
        out_specs=(pl.BlockSpec(memory_space=pl.ANY),) * 2,
        scratch_shapes=[
            vmem((tracers, blocks, LANES, LANES), F32),
            vmem((tracers * merged, LANES), F32),
            dma((1 + tracers * (blocks // group),)),
        ],
        compiler_params=pltpu.CompilerParams(vmem_limit_bytes=16 * 1024 * 1024),
        name="closing",
    )(*parts)
    return state.reshape(tracers, levels, lat_rows, lon_cells), flux


def solution(mesh):
    return jax.shard_map(
        shards,
        mesh=mesh,
        in_specs=(
            P(None, None, "lat", "lon"),
            P(None, None, "lat", "lon"),
            P(None, None, ("lat", "lon")),
            P(None, None, ("lat", "lon")),
            P(None, ("lat", "lon")),
            P(None, ("lat", "lon")),
        ),
        out_specs=(P(None, None, "lat", "lon"), P(None, "lat", "lon")),
        check_vma=False,
    )
```

```python
import functools

import jax
import jax.numpy as jnp
from jax import lax
from jax.experimental import pallas as pl
from jax.experimental.pallas import tpu as pltpu
from jax.sharding import PartitionSpec as P

MESH = pl.DeviceIdType.MESH
SUB = 8
LANES = 128
PAD = 8
F32 = jnp.float32
BF16 = jnp.bfloat16


def kernel(
    dims,
    east_hbm, north_hbm, kern_hbm, dep_hbm, cells_hbm, counts_hbm,
    gain_seg, source_seg, end_ref, flux_ref,
    kern_ref, dep_ref, cells_ref, counts_ref, edge_gain,
    weight, faces, turned, gain_levels, field, rows, rows_t, forcing,
    features, sent, stage, got_t, term_hi, term_lo, left, onehot,
    edge_out, edge_in, face_out, face_in, gain_all, rest_all,
    local_sem, slot_sem, gain_send, gain_recv,
    rest_send, rest_recv, edge_send, edge_recv, face_sem,
):
    steps, tracers, levels, lat_rows, n_lat, n_lon, slots, capacity = dims
    merged = levels * lat_rows
    blocks = merged // LANES
    seg = LANES // SUB
    half = lat_rows // 2
    fields = tracers * levels
    my_lat, my_lon = lax.axis_index("lat"), lax.axis_index("lon")
    has_up = my_lat < n_lat - 1
    has_down = my_lat > 0

    lat_ids = [lax.rem(my_lat + i, n_lat) for i in range(n_lat)]
    lon_ids = [lax.rem(my_lon + j, n_lon) for j in range(n_lon)]
    offsets = [(i, j) for i in range(n_lat) for j in range(n_lon)][1:]

    def lon_peer(k):
        return (my_lat, lon_ids[k])

    def remote(src, dst, send, recv, device):
        return pltpu.make_async_remote_copy(
            src_ref=src, dst_ref=dst, send_sem=send, recv_sem=recv,
            device_id=device, device_id_type=MESH,
        )

    small = [
        pltpu.make_async_copy(src, dst, local_sem.at[2 + i])
        for i, (src, dst) in enumerate((
            (kern_hbm, kern_ref), (dep_hbm, dep_ref), (cells_hbm, cells_ref), (counts_hbm, counts_ref),
        ))
    ]
    for copy in small:
        copy.start()
    load_east = pltpu.make_async_copy(east_hbm, weight, local_sem.at[0])
    load_east.start()
    load_north = pltpu.make_async_copy(
        north_hbm, faces.at[:, :, pl.ds(PAD, lat_rows), :], local_sem.at[1]
    )
    load_north.start()

    gain_all[...] = jnp.zeros_like(gain_all)
    rest_all[...] = jnp.zeros_like(rest_all)
    face_in[...] = jnp.zeros_like(face_in)
    edge_in[...] = jnp.zeros_like(edge_in)
    field[:, PAD - 1, :] = jnp.zeros((fields, LANES), F32)
    field[:, PAD + lat_rows, :] = jnp.zeros((fields, LANES), F32)
    barrier = pltpu.get_barrier_semaphore()
    for i, j in offsets:
        pl.semaphore_signal(
            barrier, inc=1, device_id=(lat_ids[i], lon_ids[j]), device_id_type=MESH
        )

    for copy in small:
        copy.wait()
    owners = n_lat * n_lon
    spread = (
        lax.broadcasted_iota(jnp.int32, (owners, slots), 1) // capacity
        == lax.broadcasted_iota(jnp.int32, (owners, slots), 0)
    ).astype(F32)
    counts = jnp.dot(counts_ref[...].astype(F32), spread, preferred_element_type=F32)
    within = lax.rem(lax.broadcasted_iota(jnp.int32, (steps, slots), 1), capacity).astype(F32)
    live = (within < counts).astype(F32)
    features[...] = jnp.zeros_like(features)
    dep_row = steps * levels
    cell_row = dep_row + steps * tracers
    for n in range(steps):
        features[n * levels:(n + 1) * levels, :] = kern_ref[n]
        for t in range(tracers):
            at = dep_row + n * tracers + t
            features[at:at + 1, :] = dep_ref[n, t:t + 1, :] * live[n:n + 1, :]
        features[cell_row + n:cell_row + n + 1, :] = cells_ref[n:n + 1, :].astype(F32)
    sent[...] = features[...].T.reshape(sent.shape)
    pl.semaphore_wait(barrier, len(offsets))

    for i, j in offsets:
        remote(
            sent.at[lat_ids[i] * n_lon + lon_ids[j]], stage.at[i * n_lon + j],
            slot_sem.at[0], slot_sem.at[1], (lat_ids[i], lon_ids[j]),
        ).start()
    stage[0] = sent[my_lat * n_lon + my_lon]

    load_north.wait()
    face_out[...] = faces[:, :, PAD + lat_rows - 1, :]
    up_device = (lax.rem(my_lat + 1, n_lat), my_lon)
    down_device = (lax.rem(my_lat + n_lat - 1, n_lat), my_lon)
    face_copy = remote(face_out, face_in, face_sem.at[0], face_sem.at[1], up_device)

    @pl.when(has_up)
    def _():
        face_copy.start()

    @pl.when(jnp.logical_not(has_up))
    def _():
        faces[:, :, PAD + lat_rows - 1, :] = jnp.zeros((steps, levels, LANES), F32)

    sub = lax.rem(lax.broadcasted_iota(jnp.int32, (blocks * SUB, LANES), 0), SUB)

    def ahead(x, d):
        return pltpu.roll(x, blocks * SUB - d, 0)

    def flat(x):
        return x.reshape(blocks * SUB, LANES)

    def gains(n):
        def one(b, carry):
            at = pl.ds(pl.multiple_of(b * LANES, LANES), LANES)
            east = weight[n, at, :]
            share = 1.0 / (1.0 + east)
            weight[n, at, :] = share
            turned[b] = (east * share).T
            return carry

        lax.fori_loop(0, blocks, one, 0, unroll=4)
        g = None
        for p in range(seg - 1, -1, -1):
            part = flat(turned[:, pl.ds(p, SUB, stride=seg), :])
            gain_seg[n, p] = part
            g = part if g is None else g * part
        for level, d in enumerate((1, 2, 4)):
            gain_levels[n, level] = g
            g = jnp.where(sub < SUB - d, g * ahead(g, d), g)
        gain_levels[n, 3] = g
        for b in range(blocks):
            gain_all[n, 0, b:b + 1, :] = g[b * SUB:b * SUB + 1, :]

    load_east.wait()
    gains(steps - 1)

    def gain_copies(n):
        return [
            remote(gain_all.at[n, 0], gain_all.at[n, k], gain_send.at[n, k], gain_recv.at[n, k], lon_peer(k))
            for k in range(1, n_lon)
        ]

    for copy in gain_copies(steps - 1):
        copy.start()
    arrived = stage.at[pl.ds(1, owners - 1)]
    all_slots = remote(arrived, arrived, slot_sem.at[0], slot_sem.at[1], lon_peer(1))
    all_slots.wait_recv()
    got = stage[...].reshape(slots, LANES)
    got_t[...] = got.T
    group = SUB
    tile = 16
    shift = LANES.bit_length() - 1

    def split_cell(cell):
        row = lax.shift_right_logical(cell, shift)
        upper = (row >= half).astype(jnp.int32)
        return row - half * upper, (cell & (LANES - 1)) + LANES * upper

    def deposit(n, store):
        for t in range(tracers):
            at = dep_row + n * tracers + t
            term = got_t[at:at + 1, :] * got_t[n * levels:(n + 1) * levels, :]
            high = term.astype(BF16).astype(F32)
            term_hi[t * levels:(t + 1) * levels, :] = high
            term_lo[t * levels:(t + 1) * levels, :] = term - high
        lane_cell = got_t[cell_row + n:cell_row + n + 1, :].astype(jnp.int32)
        slot_row, _ = split_cell(lane_cell)
        _, slot_col = split_cell(stage[...].reshape(slots, LANES)[
            :, cell_row + n:cell_row + n + 1].astype(jnp.int32))
        hot = (
            lax.broadcasted_iota(jnp.int32, (slots, 2 * LANES), 1) == slot_col
        ).astype(F32).astype(BF16)
        onehot[0:slots, :] = hot
        onehot[slots:2 * slots, :] = hot
        here = (
            lax.broadcasted_iota(jnp.int32, (half, slots), 0) == slot_row
        ).astype(F32).astype(BF16).reshape(half // tile, tile, slots)

        def placed(term):
            wide = jnp.broadcast_to(term, (tile, slots)).astype(BF16)
            return (here * wide[None]).reshape(half, slots)

        for c in range(fields // group):
            for i in range(group):
                at = pl.ds(c * group + i, 1)
                part = pl.ds(i * half, half)
                left[c % 2, part, 0:slots] = placed(term_hi[at, :])
                left[c % 2, part, slots:2 * slots] = placed(term_lo[at, :])
            added = jnp.dot(left[c % 2], onehot[...], preferred_element_type=F32)
            for i in range(group):
                block = added[i * half:(i + 1) * half]
                store(c * group + i, block[:, :LANES], block[:, LANES:])

    def into_field(i, low, high):
        field[i, PAD:PAD + half, :] = low
        field[i, PAD + half:PAD + lat_rows, :] = high

    def into_forcing(n):
        def store(i, low, high):
            forcing[n, i, 0:half, :] = low
            forcing[n, i, half:lat_rows, :] = high
        return store

    deposit(steps - 1, into_field)

    def edge_copies(n, t):
        to_up = remote(edge_out.at[n, 1, t], edge_in.at[n, 0, t],
                       edge_send.at[n, 1, t], edge_recv.at[n, 0, t], up_device)
        to_down = remote(edge_out.at[n, 0, t], edge_in.at[n, 1, t],
                         edge_send.at[n, 0, t], edge_recv.at[n, 1, t], down_device)
        return to_up, to_down

    def send_edges(n, t):
        to_up, to_down = edge_copies(n, t)

        @pl.when(has_up)
        def _():
            to_up.start()

        @pl.when(has_down)
        def _():
            to_down.start()

    def wait_edges(n, t):
        to_up, to_down = edge_copies(n, t)

        @pl.when(has_up)
        def _():
            to_up.wait_send()
            to_down.wait_recv()

        @pl.when(has_down)
        def _():
            to_down.wait_send()
            to_up.wait_recv()

    def rest_copies(n, t):
        return [
            remote(rest_all.at[n, t, 0], rest_all.at[n, t, k],
                   rest_send.at[n, t, k], rest_recv.at[n, t, k], lon_peer(k))
            for k in range(1, n_lon)
        ]

    def bottom_rows(t, row):
        return (pl.ds(t * merged + row, levels, stride=lat_rows), slice(None))

    def add_flux(n, t):
        surface = field[t * levels, PAD:PAD + lat_rows, :]
        flux_ref[t] = surface if n == steps - 1 else flux_ref[t] + surface

    def lat_stencil(n, t):
        def one(l, carry):
            northward = jnp.maximum(faces[n, l, PAD:PAD + lat_rows, :], 0.0)
            southward = jnp.minimum(faces[n, l, PAD - 1:PAD - 1 + lat_rows, :], 0.0)
            share = weight[n, pl.ds(pl.multiple_of(l * lat_rows, SUB), lat_rows), :]
            i = t * levels + l
            a = field[i, PAD:PAD + lat_rows, :]
            above = field[i, PAD + 1:PAD + 1 + lat_rows, :]
            below = field[i, PAD - 1:PAD - 1 + lat_rows, :]
            y = a + northward * (above - a) + southward * (a - below)
            rows[pl.ds(pl.multiple_of(i * lat_rows, SUB), lat_rows), :] = share * y
            return carry

        lax.fori_loop(0, levels, one, 0, unroll=4)

    def row_at(t, p):
        return (pl.ds(t * blocks, blocks), pl.ds(p, SUB, stride=seg), slice(None))

    def block_rest(n, t):
        for side, row in ((0, 0), (1, lat_rows - 1)):
            at = bottom_rows(t, row)
            rows[at] = rows[at] + edge_gain[n, side] * edge_in[n, side, t]

        def turn(b, carry):
            b = b + t * blocks
            rows_t[b] = rows[pl.ds(pl.multiple_of(b * LANES, LANES), LANES), :].T
            return carry

        lax.fori_loop(0, blocks, turn, 0, unroll=True)
        rest = None
        for p in range(seg - 1, -1, -1):
            part = flat(rows_t[row_at(t, p)])
            source_seg[t, p] = part
            rest = part if rest is None else gain_seg[n, p] * rest + part
        for level, d in enumerate((1, 2, 4)):
            rest = jnp.where(sub < SUB - d, rest + gain_levels[n, level] * ahead(rest, d), rest)
        for b in range(blocks):
            rest_all[n, t, 0, b:b + 1, :] = rest[b * SUB:b * SUB + 1, :]
        for copy in rest_copies(n, t):
            copy.start()
        return rest

    def finish(n, t, rest, scale):
        for copy in rest_copies(n, t):
            copy.wait()
        total = rest_all[n, t, 0]
        for k in range(1, n_lon):
            total = rest_all[n, t, k] + gain_all[n, k] * total
        closure = total * scale
        wide = jnp.concatenate(
            [jnp.broadcast_to(closure[b:b + 1, :], (SUB, LANES)) for b in range(blocks)], 0
        )
        inclusive = gain_levels[n, 3] * wide + rest
        end = jnp.where(sub == SUB - 1, wide, ahead(inclusive, 1))
        if n == 0:
            end_ref[t] = end
            return
        for p in range(seg - 1, -1, -1):
            end = gain_seg[n, p] * end + source_seg[t, p]
            rows_t[row_at(t, p)] = end.reshape(blocks, SUB, LANES)

        def turn_back(b, carry):
            b = b + t * blocks
            rows[pl.ds(pl.multiple_of(b * LANES, LANES), LANES), :] = rows_t[b].T
            return carry

        lax.fori_loop(0, blocks, turn_back, 0, unroll=True)

    def next_field(n, t):
        some = slice(t * levels, (t + 1) * levels)
        for side, row in ((0, 0), (1, lat_rows - 1)):
            edge_out[n, side, t] = rows[bottom_rows(t, row)] + forcing[n, some, row, :]
        send_edges(n, t)

        def add(l, carry):
            i = t * levels + l
            solved = rows[pl.ds(pl.multiple_of(i * lat_rows, SUB), lat_rows), :]
            field[i, PAD:PAD + lat_rows, :] = solved + forcing[n, i]
            return carry

        lax.fori_loop(0, levels, add, 0, unroll=4)
        add_flux(n, t)
        lat_stencil(n, t)

    last = steps - 1
    for t in range(tracers):
        some = slice(t * levels, (t + 1) * levels)
        edge_out[last, 0, t] = field[some, PAD, :]
        edge_out[last, 1, t] = field[some, PAD + lat_rows - 1, :]
        send_edges(last, t)
    for m in range(steps - 2, -1, -1):
        gains(m)
        for copy in gain_copies(m):
            copy.start()

    @pl.when(has_down)
    def _():
        face_copy.wait_recv()

    @pl.when(has_up)
    def _():
        face_copy.wait_send()

    faces[:, :, PAD - 1, :] = face_in[...]
    for n in range(steps):
        low = weight[n, pl.ds(0, levels, stride=lat_rows), :]
        high = weight[n, pl.ds(lat_rows - 1, levels, stride=lat_rows), :]
        edge_gain[n, 0] = -jnp.minimum(face_in[n], 0.0) * low
        edge_gain[n, 1] = jnp.maximum(faces[n, :, PAD + lat_rows - 1, :], 0.0) * high
    for t in range(tracers):
        add_flux(last, t)
        lat_stencil(last, t)

    for n in range(last, -1, -1):
        rests = []
        for t in range(tracers):
            wait_edges(n, t)
            rests.append(block_rest(n, t))
        if n == last:
            for m in range(steps - 2, -1, -1):
                deposit(m, into_forcing(m))
        for copy in gain_copies(n):
            copy.wait()
        whole = gain_all[n, 0]
        for k in range(1, n_lon):
            whole = whole * gain_all[n, k]
        scale = 1.0 / (1.0 - whole)
        for t in range(tracers):
            finish(n, t, rests[t], scale)
            if n > 0:
                next_field(n - 1, t)
    all_slots.wait_send()


def closing(
    dims, gain_seg, source_seg, end_ref, flux_ref, out_hbm, flux_hbm, rows_t, rows, sems
):
    tracers, blocks, group = dims
    seg = LANES // SUB
    flux_copy = pltpu.make_async_copy(flux_ref, flux_hbm, sems.at[0])
    flux_copy.start()
    copies = [flux_copy]
    for t in range(tracers):
        end = end_ref[t]
        for p in range(seg - 1, -1, -1):
            end = gain_seg[0, p] * end + source_seg[t, p]
            rows_t[t, :, pl.ds(p, SUB, stride=seg), :] = end.reshape(blocks, SUB, LANES)
        for first in range(0, blocks, group):
            for b in range(first, first + group):
                at = (t * blocks + b) * LANES
                rows[at:at + LANES, :] = rows_t[t, b].T
            some = pl.ds((t * blocks + first) * LANES, group * LANES)
            copies.append(pltpu.make_async_copy(rows.at[some], out_hbm.at[some], sems.at[len(copies)]))
            copies[-1].start()
    for copy in copies:
        copy.wait()


def shards(east_courant, north_courant, kernels, departures, cells, counts):
    steps, levels, lat_rows, lon_cells = east_courant.shape
    tracers = departures.shape[1]
    n_lat, n_lon = lax.axis_size("lat"), lax.axis_size("lon")
    owners = n_lat * n_lon
    slots = cells.shape[1]
    capacity = slots // owners
    merged = levels * lat_rows
    blocks = merged // LANES
    padded = -(-blocks // SUB) * SUB
    fields = tracers * levels
    dims = (steps, tracers, levels, lat_rows, n_lat, n_lon, slots, capacity)
    vmem = pltpu.VMEM
    dma = pltpu.SemaphoreType.DMA
    near = pl.BlockSpec(memory_space=pltpu.VMEM)
    far = pl.BlockSpec(memory_space=pltpu.HBM)
    seg = LANES // SUB
    parts = pl.pallas_call(
        functools.partial(kernel, dims),
        out_shape=(
            vmem((steps, seg, blocks * SUB, LANES), F32),
            vmem((tracers, seg, blocks * SUB, LANES), F32),
            vmem((tracers, blocks * SUB, LANES), F32),
            vmem((tracers, lat_rows, lon_cells), F32),
        ),
        in_specs=[far] * 6,
        out_specs=(near,) * 4,
        scratch_shapes=[
            vmem(kernels.shape, F32),
            vmem(departures.shape, F32),
            vmem(cells.shape, jnp.int32),
            vmem(counts.shape, jnp.int32),
            vmem((steps, 2, levels, LANES), F32),
            vmem((steps, merged, LANES), F32),
            vmem((steps, levels, lat_rows + PAD, LANES), F32),
            vmem((blocks, LANES, LANES), F32),
            vmem((steps, 4, blocks * SUB, LANES), F32),
            vmem((fields, lat_rows + 2 * PAD, LANES), F32),
            vmem((tracers * merged, LANES), F32),
            vmem((tracers * blocks, LANES, LANES), F32),
            vmem((max(steps - 1, 1), fields, lat_rows, LANES), F32),
            vmem((LANES, slots), F32),
            vmem((owners, capacity, LANES), F32),
            vmem((owners, capacity, LANES), F32),
            vmem((LANES, slots), F32),
            vmem((fields, slots), F32),
            vmem((fields, slots), F32),
            vmem((2, SUB * lat_rows // 2, 2 * slots), BF16),
            vmem((2 * slots, 2 * LANES), BF16),
            vmem((steps, 2, tracers, levels, LANES), F32),
            vmem((steps, 2, tracers, levels, LANES), F32),
            vmem((steps, levels, LANES), F32),
            vmem((steps, levels, LANES), F32),
            vmem((steps, n_lon, padded, LANES), F32),
            vmem((steps, tracers, n_lon, padded, LANES), F32),
            dma((6,)),
            dma((2,)),
            dma((steps, n_lon)), dma((steps, n_lon)),
            dma((steps, tracers, n_lon)), dma((steps, tracers, n_lon)),
            dma((steps, 2, tracers)), dma((steps, 2, tracers)),
            dma((2,)),
        ],
        compiler_params=pltpu.CompilerParams(
            collective_id=0, has_side_effects=True, vmem_limit_bytes=40 * 1024 * 1024
        ),
        name="adjoint_window",
    )(
        *(
            pltpu.with_memory_space_constraint(x, pltpu.HBM)
            for x in (
                east_courant.reshape(steps, merged, lon_cells), north_courant,
                kernels, departures, cells, counts,
            )
        )
    )
    group = 4 if blocks % 4 == 0 else 1
    state, flux = pl.pallas_call(
        functools.partial(closing, (tracers, blocks, group)),
        out_shape=(
            jax.ShapeDtypeStruct((tracers * merged, lon_cells), F32),
            jax.ShapeDtypeStruct((tracers, lat_rows, lon_cells), F32),
        ),
        in_specs=[near] * 4,
        out_specs=(pl.BlockSpec(memory_space=pl.ANY),) * 2,
        scratch_shapes=[
            vmem((tracers, blocks, LANES, LANES), F32),
            vmem((tracers * merged, LANES), F32),
            dma((1 + tracers * (blocks // group),)),
        ],
        compiler_params=pltpu.CompilerParams(vmem_limit_bytes=16 * 1024 * 1024),
        name="closing",
    )(*parts)
    return state.reshape(tracers, levels, lat_rows, lon_cells), flux


def solution(mesh):
    return jax.shard_map(
        shards,
        mesh=mesh,
        in_specs=(
            P(None, None, "lat", "lon"),
            P(None, None, "lat", "lon"),
            P(None, None, ("lat", "lon")),
            P(None, None, ("lat", "lon")),
            P(None, ("lat", "lon")),
            P(None, ("lat", "lon")),
        ),
        out_specs=(P(None, None, "lat", "lon"), P(None, "lat", "lon")),
        check_vma=False,
    )
```

```python
import functools

import jax
import jax.numpy as jnp
from jax import lax
from jax.experimental import pallas as pl
from jax.experimental.pallas import tpu as pltpu
from jax.sharding import PartitionSpec as P

MESH = pl.DeviceIdType.MESH
SUB = 8
LANES = 128
PAD = 8
F32 = jnp.float32
BF16 = jnp.bfloat16


def kernel(
    dims,
    east_hbm, north_hbm, kern_hbm, dep_hbm, cells_hbm, counts_hbm,
    gain_seg, source_seg, end_ref, flux_ref,
    kern_ref, dep_ref, cells_ref, counts_ref, edge_gain,
    weight, faces, turned, gain_levels, field, rows, rows_t, forcing,
    features, sent, stage, got_t, term_hi, term_lo, left, onehot,
    edge_out, edge_in, face_out, face_in, gain_all, rest_all,
    local_sem, slot_sem, gain_send, gain_recv,
    rest_send, rest_recv, edge_send, edge_recv, face_sem,
):
    steps, tracers, levels, lat_rows, n_lat, n_lon, slots, capacity = dims
    merged = levels * lat_rows
    blocks = merged // LANES
    seg = LANES // SUB
    half = lat_rows // 2
    fields = tracers * levels
    my_lat, my_lon = lax.axis_index("lat"), lax.axis_index("lon")
    has_up = my_lat < n_lat - 1
    has_down = my_lat > 0

    lat_ids = [lax.rem(my_lat + i, n_lat) for i in range(n_lat)]
    lon_ids = [lax.rem(my_lon + j, n_lon) for j in range(n_lon)]
    offsets = [(i, j) for i in range(n_lat) for j in range(n_lon)][1:]

    def lon_peer(k):
        return (my_lat, lon_ids[k])

    def remote(src, dst, send, recv, device):
        return pltpu.make_async_remote_copy(
            src_ref=src, dst_ref=dst, send_sem=send, recv_sem=recv,
            device_id=device, device_id_type=MESH,
        )

    small = [
        pltpu.make_async_copy(src, dst, local_sem.at[2 + i])
        for i, (src, dst) in enumerate((
            (kern_hbm, kern_ref), (dep_hbm, dep_ref), (cells_hbm, cells_ref), (counts_hbm, counts_ref),
        ))
    ]
    for copy in small:
        copy.start()
    load_east = pltpu.make_async_copy(east_hbm, weight, local_sem.at[0])
    load_east.start()
    load_north = pltpu.make_async_copy(
        north_hbm, faces.at[:, :, pl.ds(PAD, lat_rows), :], local_sem.at[1]
    )
    load_north.start()

    gain_all[...] = jnp.zeros_like(gain_all)
    rest_all[...] = jnp.zeros_like(rest_all)
    face_in[...] = jnp.zeros_like(face_in)
    edge_in[...] = jnp.zeros_like(edge_in)
    field[:, PAD - 1, :] = jnp.zeros((fields, LANES), F32)
    field[:, PAD + lat_rows, :] = jnp.zeros((fields, LANES), F32)
    barrier = pltpu.get_barrier_semaphore()
    for i, j in offsets:
        pl.semaphore_signal(
            barrier, inc=1, device_id=(lat_ids[i], lon_ids[j]), device_id_type=MESH
        )

    for copy in small:
        copy.wait()
    owners = n_lat * n_lon
    spread = (
        lax.broadcasted_iota(jnp.int32, (owners, slots), 1) // capacity
        == lax.broadcasted_iota(jnp.int32, (owners, slots), 0)
    ).astype(F32)
    counts = jnp.dot(counts_ref[...].astype(F32), spread, preferred_element_type=F32)
    within = lax.rem(lax.broadcasted_iota(jnp.int32, (steps, slots), 1), capacity).astype(F32)
    live = (within < counts).astype(F32)
    features[...] = jnp.zeros_like(features)
    dep_row = steps * levels
    cell_row = dep_row + steps * tracers
    for n in range(steps):
        features[n * levels:(n + 1) * levels, :] = kern_ref[n]
        for t in range(tracers):
            at = dep_row + n * tracers + t
            features[at:at + 1, :] = dep_ref[n, t:t + 1, :] * live[n:n + 1, :]
        features[cell_row + n:cell_row + n + 1, :] = cells_ref[n:n + 1, :].astype(F32)
    sent[...] = features[...].T.reshape(sent.shape)
    pl.semaphore_wait(barrier, len(offsets))

    for i, j in offsets:
        remote(
            sent.at[lat_ids[i] * n_lon + lon_ids[j]], stage.at[i * n_lon + j],
            slot_sem.at[0], slot_sem.at[1], (lat_ids[i], lon_ids[j]),
        ).start()
    stage[0] = sent[my_lat * n_lon + my_lon]

    load_north.wait()
    face_out[...] = faces[:, :, PAD + lat_rows - 1, :]
    up_device = (lax.rem(my_lat + 1, n_lat), my_lon)
    down_device = (lax.rem(my_lat + n_lat - 1, n_lat), my_lon)
    face_copy = remote(face_out, face_in, face_sem.at[0], face_sem.at[1], up_device)

    @pl.when(has_up)
    def _():
        face_copy.start()

    @pl.when(jnp.logical_not(has_up))
    def _():
        faces[:, :, PAD + lat_rows - 1, :] = jnp.zeros((steps, levels, LANES), F32)

    sub = lax.rem(lax.broadcasted_iota(jnp.int32, (blocks * SUB, LANES), 0), SUB)

    def ahead(x, d):
        return pltpu.roll(x, blocks * SUB - d, 0)

    def flat(x):
        return x.reshape(blocks * SUB, LANES)

    def gains(n):
        def one(b, carry):
            at = pl.ds(pl.multiple_of(b * LANES, LANES), LANES)
            east = weight[n, at, :]
            share = 1.0 / (1.0 + east)
            weight[n, at, :] = share
            turned[b] = (east * share).T
            return carry

        lax.fori_loop(0, blocks, one, 0, unroll=4)
        g = None
        for p in range(seg - 1, -1, -1):
            part = flat(turned[:, pl.ds(p, SUB, stride=seg), :])
            gain_seg[n, p] = part
            g = part if g is None else g * part
        for level, d in enumerate((1, 2, 4)):
            gain_levels[n, level] = g
            g = jnp.where(sub < SUB - d, g * ahead(g, d), g)
        gain_levels[n, 3] = g
        for b in range(blocks):
            gain_all[n, 0, b:b + 1, :] = g[b * SUB:b * SUB + 1, :]

    load_east.wait()
    gains(steps - 1)

    def gain_copies(n):
        return [
            remote(gain_all.at[n, 0], gain_all.at[n, k], gain_send.at[n, k], gain_recv.at[n, k], lon_peer(k))
            for k in range(1, n_lon)
        ]

    for copy in gain_copies(steps - 1):
        copy.start()
    for m in range(steps - 2, -1, -1):
        gains(m)
        for copy in gain_copies(m):
            copy.start()
    arrived = stage.at[pl.ds(1, owners - 1)]
    all_slots = remote(arrived, arrived, slot_sem.at[0], slot_sem.at[1], lon_peer(1))
    all_slots.wait_recv()
    got = stage[...].reshape(slots, LANES)
    got_t[...] = got.T
    group = SUB
    tile = 16
    shift = LANES.bit_length() - 1

    def split_cell(cell):
        row = lax.shift_right_logical(cell, shift)
        upper = (row >= half).astype(jnp.int32)
        return row - half * upper, (cell & (LANES - 1)) + LANES * upper

    def deposit(n, store):
        for t in range(tracers):
            at = dep_row + n * tracers + t
            term = got_t[at:at + 1, :] * got_t[n * levels:(n + 1) * levels, :]
            high = term.astype(BF16).astype(F32)
            term_hi[t * levels:(t + 1) * levels, :] = high
            term_lo[t * levels:(t + 1) * levels, :] = term - high
        lane_cell = got_t[cell_row + n:cell_row + n + 1, :].astype(jnp.int32)
        slot_row, _ = split_cell(lane_cell)
        _, slot_col = split_cell(stage[...].reshape(slots, LANES)[
            :, cell_row + n:cell_row + n + 1].astype(jnp.int32))
        hot = (
            lax.broadcasted_iota(jnp.int32, (slots, 2 * LANES), 1) == slot_col
        ).astype(F32).astype(BF16)
        onehot[0:slots, :] = hot
        onehot[slots:2 * slots, :] = hot
        here = (
            lax.broadcasted_iota(jnp.int32, (half, slots), 0) == slot_row
        ).astype(F32).astype(BF16).reshape(half // tile, tile, slots)

        def placed(term):
            wide = jnp.broadcast_to(term, (tile, slots)).astype(BF16)
            return (here * wide[None]).reshape(half, slots)

        for c in range(fields // group):
            for i in range(group):
                at = pl.ds(c * group + i, 1)
                part = pl.ds(i * half, half)
                left[c % 2, part, 0:slots] = placed(term_hi[at, :])
                left[c % 2, part, slots:2 * slots] = placed(term_lo[at, :])
            added = jnp.dot(left[c % 2], onehot[...], preferred_element_type=F32)
            for i in range(group):
                block = added[i * half:(i + 1) * half]
                store(c * group + i, block[:, :LANES], block[:, LANES:])

    def into_field(i, low, high):
        field[i, PAD:PAD + half, :] = low
        field[i, PAD + half:PAD + lat_rows, :] = high

    def into_forcing(n):
        def store(i, low, high):
            forcing[n, i, 0:half, :] = low
            forcing[n, i, half:lat_rows, :] = high
        return store

    deposit(steps - 1, into_field)

    def edge_copies(n, t):
        to_up = remote(edge_out.at[n, 1, t], edge_in.at[n, 0, t],
                       edge_send.at[n, 1, t], edge_recv.at[n, 0, t], up_device)
        to_down = remote(edge_out.at[n, 0, t], edge_in.at[n, 1, t],
                         edge_send.at[n, 0, t], edge_recv.at[n, 1, t], down_device)
        return to_up, to_down

    def send_edges(n, t):
        to_up, to_down = edge_copies(n, t)

        @pl.when(has_up)
        def _():
            to_up.start()

        @pl.when(has_down)
        def _():
            to_down.start()

    def wait_edges(n, t):
        to_up, to_down = edge_copies(n, t)

        @pl.when(has_up)
        def _():
            to_up.wait_send()
            to_down.wait_recv()

        @pl.when(has_down)
        def _():
            to_down.wait_send()
            to_up.wait_recv()

    def rest_copies(n, t):
        return [
            remote(rest_all.at[n, t, 0], rest_all.at[n, t, k],
                   rest_send.at[n, t, k], rest_recv.at[n, t, k], lon_peer(k))
            for k in range(1, n_lon)
        ]

    def bottom_rows(t, row):
        return (pl.ds(t * merged + row, levels, stride=lat_rows), slice(None))

    def add_flux(n, t):
        surface = field[t * levels, PAD:PAD + lat_rows, :]
        flux_ref[t] = surface if n == steps - 1 else flux_ref[t] + surface

    def lat_stencil(n, t):
        def one(l, carry):
            northward = jnp.maximum(faces[n, l, PAD:PAD + lat_rows, :], 0.0)
            southward = jnp.minimum(faces[n, l, PAD - 1:PAD - 1 + lat_rows, :], 0.0)
            share = weight[n, pl.ds(pl.multiple_of(l * lat_rows, SUB), lat_rows), :]
            i = t * levels + l
            a = field[i, PAD:PAD + lat_rows, :]
            above = field[i, PAD + 1:PAD + 1 + lat_rows, :]
            below = field[i, PAD - 1:PAD - 1 + lat_rows, :]
            y = a + northward * (above - a) + southward * (a - below)
            rows[pl.ds(pl.multiple_of(i * lat_rows, SUB), lat_rows), :] = share * y
            return carry

        lax.fori_loop(0, levels, one, 0, unroll=4)

    def row_at(t, p):
        return (pl.ds(t * blocks, blocks), pl.ds(p, SUB, stride=seg), slice(None))

    def block_rest(n, t):
        for side, row in ((0, 0), (1, lat_rows - 1)):
            at = bottom_rows(t, row)
            rows[at] = rows[at] + edge_gain[n, side] * edge_in[n, side, t]

        def turn(b, carry):
            b = b + t * blocks
            rows_t[b] = rows[pl.ds(pl.multiple_of(b * LANES, LANES), LANES), :].T
            return carry

        lax.fori_loop(0, blocks, turn, 0, unroll=True)
        rest = None
        for p in range(seg - 1, -1, -1):
            part = flat(rows_t[row_at(t, p)])
            source_seg[t, p] = part
            rest = part if rest is None else gain_seg[n, p] * rest + part
        for level, d in enumerate((1, 2, 4)):
            rest = jnp.where(sub < SUB - d, rest + gain_levels[n, level] * ahead(rest, d), rest)
        for b in range(blocks):
            rest_all[n, t, 0, b:b + 1, :] = rest[b * SUB:b * SUB + 1, :]
        for copy in rest_copies(n, t):
            copy.start()
        return rest

    def finish(n, t, rest, scale):
        for copy in rest_copies(n, t):
            copy.wait()
        total = rest_all[n, t, 0]
        for k in range(1, n_lon):
            total = rest_all[n, t, k] + gain_all[n, k] * total
        closure = total * scale
        wide = jnp.concatenate(
            [jnp.broadcast_to(closure[b:b + 1, :], (SUB, LANES)) for b in range(blocks)], 0
        )
        inclusive = gain_levels[n, 3] * wide + rest
        end = jnp.where(sub == SUB - 1, wide, ahead(inclusive, 1))
        if n == 0:
            end_ref[t] = end
            return
        for p in range(seg - 1, -1, -1):
            end = gain_seg[n, p] * end + source_seg[t, p]
            rows_t[row_at(t, p)] = end.reshape(blocks, SUB, LANES)

        def turn_back(b, carry):
            b = b + t * blocks
            rows[pl.ds(pl.multiple_of(b * LANES, LANES), LANES), :] = rows_t[b].T
            return carry

        lax.fori_loop(0, blocks, turn_back, 0, unroll=True)

    def next_field(n, t):
        some = slice(t * levels, (t + 1) * levels)
        for side, row in ((0, 0), (1, lat_rows - 1)):
            edge_out[n, side, t] = rows[bottom_rows(t, row)] + forcing[n, some, row, :]
        send_edges(n, t)

        def add(l, carry):
            i = t * levels + l
            solved = rows[pl.ds(pl.multiple_of(i * lat_rows, SUB), lat_rows), :]
            field[i, PAD:PAD + lat_rows, :] = solved + forcing[n, i]
            return carry

        lax.fori_loop(0, levels, add, 0, unroll=4)
        add_flux(n, t)
        lat_stencil(n, t)

    last = steps - 1
    for t in range(tracers):
        some = slice(t * levels, (t + 1) * levels)
        edge_out[last, 0, t] = field[some, PAD, :]
        edge_out[last, 1, t] = field[some, PAD + lat_rows - 1, :]
        send_edges(last, t)
    @pl.when(has_down)
    def _():
        face_copy.wait_recv()

    @pl.when(has_up)
    def _():
        face_copy.wait_send()

    faces[:, :, PAD - 1, :] = face_in[...]
    for n in range(steps):
        low = weight[n, pl.ds(0, levels, stride=lat_rows), :]
        high = weight[n, pl.ds(lat_rows - 1, levels, stride=lat_rows), :]
        edge_gain[n, 0] = -jnp.minimum(face_in[n], 0.0) * low
        edge_gain[n, 1] = jnp.maximum(faces[n, :, PAD + lat_rows - 1, :], 0.0) * high
    for t in range(tracers):
        add_flux(last, t)
        lat_stencil(last, t)

    for n in range(last, -1, -1):
        rests = []
        for t in range(tracers):
            wait_edges(n, t)
            rests.append(block_rest(n, t))
        if n == last:
            for m in range(steps - 2, -1, -1):
                deposit(m, into_forcing(m))
        for copy in gain_copies(n):
            copy.wait()
        whole = gain_all[n, 0]
        for k in range(1, n_lon):
            whole = whole * gain_all[n, k]
        scale = 1.0 / (1.0 - whole)
        for t in range(tracers):
            finish(n, t, rests[t], scale)
            if n > 0:
                next_field(n - 1, t)
    all_slots.wait_send()


def closing(
    dims, gain_seg, source_seg, end_ref, flux_ref, out_hbm, flux_hbm, rows_t, rows, sems
):
    tracers, blocks, group = dims
    seg = LANES // SUB
    flux_copy = pltpu.make_async_copy(flux_ref, flux_hbm, sems.at[0])
    flux_copy.start()
    copies = [flux_copy]
    for t in range(tracers):
        end = end_ref[t]
        for p in range(seg - 1, -1, -1):
            end = gain_seg[0, p] * end + source_seg[t, p]
            rows_t[t, :, pl.ds(p, SUB, stride=seg), :] = end.reshape(blocks, SUB, LANES)
        for first in range(0, blocks, group):
            for b in range(first, first + group):
                at = (t * blocks + b) * LANES
                rows[at:at + LANES, :] = rows_t[t, b].T
            some = pl.ds((t * blocks + first) * LANES, group * LANES)
            copies.append(pltpu.make_async_copy(rows.at[some], out_hbm.at[some], sems.at[len(copies)]))
            copies[-1].start()
    for copy in copies:
        copy.wait()


def shards(east_courant, north_courant, kernels, departures, cells, counts):
    steps, levels, lat_rows, lon_cells = east_courant.shape
    tracers = departures.shape[1]
    n_lat, n_lon = lax.axis_size("lat"), lax.axis_size("lon")
    owners = n_lat * n_lon
    slots = cells.shape[1]
    capacity = slots // owners
    merged = levels * lat_rows
    blocks = merged // LANES
    padded = -(-blocks // SUB) * SUB
    fields = tracers * levels
    dims = (steps, tracers, levels, lat_rows, n_lat, n_lon, slots, capacity)
    vmem = pltpu.VMEM
    dma = pltpu.SemaphoreType.DMA
    near = pl.BlockSpec(memory_space=pltpu.VMEM)
    far = pl.BlockSpec(memory_space=pltpu.HBM)
    seg = LANES // SUB
    parts = pl.pallas_call(
        functools.partial(kernel, dims),
        out_shape=(
            vmem((steps, seg, blocks * SUB, LANES), F32),
            vmem((tracers, seg, blocks * SUB, LANES), F32),
            vmem((tracers, blocks * SUB, LANES), F32),
            vmem((tracers, lat_rows, lon_cells), F32),
        ),
        in_specs=[far] * 6,
        out_specs=(near,) * 4,
        scratch_shapes=[
            vmem(kernels.shape, F32),
            vmem(departures.shape, F32),
            vmem(cells.shape, jnp.int32),
            vmem(counts.shape, jnp.int32),
            vmem((steps, 2, levels, LANES), F32),
            vmem((steps, merged, LANES), F32),
            vmem((steps, levels, lat_rows + PAD, LANES), F32),
            vmem((blocks, LANES, LANES), F32),
            vmem((steps, 4, blocks * SUB, LANES), F32),
            vmem((fields, lat_rows + 2 * PAD, LANES), F32),
            vmem((tracers * merged, LANES), F32),
            vmem((tracers * blocks, LANES, LANES), F32),
            vmem((max(steps - 1, 1), fields, lat_rows, LANES), F32),
            vmem((LANES, slots), F32),
            vmem((owners, capacity, LANES), F32),
            vmem((owners, capacity, LANES), F32),
            vmem((LANES, slots), F32),
            vmem((fields, slots), F32),
            vmem((fields, slots), F32),
            vmem((2, SUB * lat_rows // 2, 2 * slots), BF16),
            vmem((2 * slots, 2 * LANES), BF16),
            vmem((steps, 2, tracers, levels, LANES), F32),
            vmem((steps, 2, tracers, levels, LANES), F32),
            vmem((steps, levels, LANES), F32),
            vmem((steps, levels, LANES), F32),
            vmem((steps, n_lon, padded, LANES), F32),
            vmem((steps, tracers, n_lon, padded, LANES), F32),
            dma((6,)),
            dma((2,)),
            dma((steps, n_lon)), dma((steps, n_lon)),
            dma((steps, tracers, n_lon)), dma((steps, tracers, n_lon)),
            dma((steps, 2, tracers)), dma((steps, 2, tracers)),
            dma((2,)),
        ],
        compiler_params=pltpu.CompilerParams(
            collective_id=0, has_side_effects=True, vmem_limit_bytes=40 * 1024 * 1024
        ),
        name="adjoint_window",
    )(
        *(
            pltpu.with_memory_space_constraint(x, pltpu.HBM)
            for x in (
                east_courant.reshape(steps, merged, lon_cells), north_courant,
                kernels, departures, cells, counts,
            )
        )
    )
    group = 4 if blocks % 4 == 0 else 1
    state, flux = pl.pallas_call(
        functools.partial(closing, (tracers, blocks, group)),
        out_shape=(
            jax.ShapeDtypeStruct((tracers * merged, lon_cells), F32),
            jax.ShapeDtypeStruct((tracers, lat_rows, lon_cells), F32),
        ),
        in_specs=[near] * 4,
        out_specs=(pl.BlockSpec(memory_space=pl.ANY),) * 2,
        scratch_shapes=[
            vmem((tracers, blocks, LANES, LANES), F32),
            vmem((tracers * merged, LANES), F32),
            dma((1 + tracers * (blocks // group),)),
        ],
        compiler_params=pltpu.CompilerParams(vmem_limit_bytes=16 * 1024 * 1024),
        name="closing",
    )(*parts)
    return state.reshape(tracers, levels, lat_rows, lon_cells), flux


def solution(mesh):
    return jax.shard_map(
        shards,
        mesh=mesh,
        in_specs=(
            P(None, None, "lat", "lon"),
            P(None, None, "lat", "lon"),
            P(None, None, ("lat", "lon")),
            P(None, None, ("lat", "lon")),
            P(None, ("lat", "lon")),
            P(None, ("lat", "lon")),
        ),
        out_specs=(P(None, None, "lat", "lon"), P(None, "lat", "lon")),
        check_vma=False,
    )
```
